256 devices in a mesh: ctx: 32 (over y, x, z_lo), exp: 8 (over z_hi, core).
Axes of the slice: x: 4, y: 4, z: 8 (z_hi: 4, z_lo: 2; z = z_hi * 2 + z_lo), core: 2. Of those that a mesh axis runs over, the one named last changes fastest.
Arguments:
- queries: bfloat16 [4096, 32, 576], P('ctx', 'exp'), may hold values from -32 to 32
- key_latents: bfloat16 [2048, 576], P('ctx'), may hold values from -8 to 8
- query_pos: int32 [4096], P('ctx'), may hold values from 1 to 2047
- value_up: bfloat16 [32, 512, 128], P('exp'), may hold values from -0.25 to 0.25
- out_proj: bfloat16 [32, 128, 2304], P('exp'), may hold values from -0.09375 to 0.09375
- stream: bfloat16 [4096, 2304], P('ctx'), may hold values from -6 to 6
- norm_gain: bfloat16 [2304], replicated, may hold values from 0.099609375 to 1.8984375
- expert_ids: int32 [4096, 8], P('ctx'), may hold values from 0 to 255, all different within a row; in each aligned block of 128 rows (0 to 127, 128 to 255, ...) at most 8 rows name the same one
- gate_weights: float32 [4096, 8], P('ctx'), may hold values from 0.05 to 0.4
- w_gate: bfloat16 [256, 2304, 512], P(('ctx', 'exp')), may hold values from -0.125 to 0.125
- w_up: bfloat16 [256, 2304, 512], P(('ctx', 'exp')), may hold values from -0.125 to 0.125
- w_down: bfloat16 [256, 512, 2304], P(('ctx', 'exp')), may hold values from -0.25 to 0.25
- out_grad: bfloat16 [4096, 2304], P('ctx'), may hold values from -6 to 6
Outputs:
- stream_grad: bfloat16 [4096, 2304], P('ctx')
- query_grad: bfloat16 [4096, 32, 576], P('ctx', 'exp')
- key_grad: bfloat16 [2048, 576], P('ctx')
The draws below stay inside these ranges and needn't reach their ends.
Inputs may be any that keep to these rules, and one draw needn't show every extreme that they name: `expert_ids`: in the rows of one index of ctx no expert is named by more than 8 rows, a bound that some block reaches; a row names 8 different experts. Row r sees context tokens 0 to query_pos[r].
All inputs are finite; a program needn't handle non-finite values.
Results may differ from the reference program's by a relative error of at most 0.015.
Values may be sent and summed in bfloat16 or wider, within the bound.
No kernel may reach another device: no remote copies, remote signals or barrier semaphores. Data moves between devices by JAX's collectives and lax.ppermute only.
A program may use at most 128 MiB of HBM per device.

```python
import math
import jax
import jax.numpy as jnp
import numpy as np
from jax import lax

D = 2304
LAT = 512
ROPE = 64
VHEAD = 128
FF = 512
TOP = 8
Q_DEV = 128
KW = 576
HEADS = 32
EXPERTS = 256
Q_ROWS = 4096
KEYS = 2048
CAP = 8
N_CTX = 32


def shared_keys(key):
    return jnp.clip(jax.random.normal(key, (KEYS, KW), jnp.float32), -6.0, 6.0)


def draw_key_latents(key, part):
    base = shared_keys(key)
    return base.astype(jnp.bfloat16)


def draw_queries(key, part):
    key = jax.random.fold_in(key, 12)
    first = jax.random.fold_in(key, 0)
    drawn = jnp.clip(jax.random.normal(first, (Q_ROWS, HEADS, KW), jnp.float32), -6.0, 6.0)
    return drawn.astype(jnp.bfloat16)


def place_ends(values, stream_key, low, largest):
    longest = values.shape.index(max(values.shape))
    spots = []
    for shift in (0, 1):
        where = [jax.random.randint(jax.random.fold_in(stream_key, axis), (), 0, length) for axis, length in enumerate(values.shape)]
        where[longest] = (where[longest] + shift) % values.shape[longest]
        spots.append(tuple(where))
    return values.at[spots[0]].set(low).at[spots[1]].set(largest)


def levels(stream_key, extent, pieces, least, largest):
    loudness, own = 1.0, jax.random.fold_in(stream_key, 6)
    for position, shards_of in pieces:
        draws = jnp.exp(jax.random.uniform(jax.random.fold_in(own, position), (shards_of,), jnp.float32, least / len(pieces), largest / len(pieces)))
        loudness = loudness * jnp.repeat(draws, extent[position] // shards_of).reshape([-1 if axis == position else 1 for axis in range(len(extent))])
    return loudness


def assign_block(own_key, own, number, rows, amount, top, most, lean):
    ranking = jax.random.permutation(own_key, amount)
    crowded, usual = load_shares(amount, rows * top, most, lean, True), load_shares(amount, rows * top, most, lean, False)
    places = jnp.arange(amount)

    def named(sizes, rotation):
        used = int((sizes > 0).sum())
        fixed = max(1, used // 4)
        moved = fixed + (places - fixed + rotation * (used - fixed)) % max(1, amount - fixed)
        return jnp.zeros((amount,), jnp.int32).at[ranking[jnp.where(places < fixed, places, moved)]].set(jnp.asarray(sizes, jnp.int32))

    sizes = jnp.where(number % 4 == 0, named(crowded, number // 4), named(usual, number - number // 4 - 1))
    mixed = jax.random.permutation(jax.random.fold_in(own, 3), amount)
    giver, taker = mixed[0:amount // 2 * 2:2], mixed[1:amount // 2 * 2:2]
    slack = jnp.minimum(sizes[giver] - 1, most - sizes[taker]) // 2
    slack = jnp.where((giver == ranking[0]) | (taker == ranking[0]) | (sizes[taker] == 0), 0, jnp.maximum(slack, 0))
    moved = jax.random.randint(jax.random.fold_in(own, 4), (amount // 2,), 0, 1 << 20) % (slack + 1)
    sizes = sizes.at[giver].add(-moved).at[taker].add(moved)
    members = jnp.searchsorted(jnp.cumsum(sizes), jnp.arange(rows * top), side="right").astype(jnp.int32)
    grid = members.reshape(top, rows).T
    grid = grid[jax.random.permutation(jax.random.fold_in(own, 1), rows)]
    rotation = jax.random.randint(jax.random.fold_in(own, 2), (rows, 1), 0, top)
    return jnp.take_along_axis(grid, (jnp.arange(top)[None, :] + rotation) % top, axis=1)


def load_shares(amount, total, bound, skew, full):
    loads = [(1 << 20) // math.isqrt(rank ** skew) + 1 for rank in range(1, amount + 1)]
    largest = bound if full else min(bound, max(-(-total // amount), total * loads[0] // sum(loads)))
    least = 1 if total - largest >= amount - 1 else 0
    given, surplus = [largest] + [least] * (amount - 1), total - largest - least * (amount - 1)
    while surplus > 0:
        candidates = [i for i in range(1, amount) if given[i] < largest] or [i for i in range(1, amount) if given[i] < bound]
        whole, remaining = sum([loads[i] for i in candidates]), surplus
        for i in candidates:
            extra = min(bound - given[i], max(1, remaining * loads[i] // whole), surplus)
            given[i] = given[i] + extra
            surplus = surplus - extra
    return np.array(given)


def bell_draw(stream_key, dims, scale, bound, shards=(), held_as=jnp.bfloat16):
    entries = scale * jax.random.normal(stream_key, dims, jnp.float32)
    if shards:
        entries = entries * levels(stream_key, dims, shards, -0.22, 0.18)
    return jnp.clip(entries, -bound, bound).astype(held_as)


def setup_inputs(seed: int = 0) -> dict:
    keys = jax.random.split(jax.random.key(seed), 14)
    queries = draw_queries(jax.random.fold_in(keys[13], 71), 0)
    key_latents = draw_key_latents(jax.random.fold_in(keys[13], 71), 0)
    query_pos = place_ends(jax.random.randint(keys[2], (Q_ROWS,), 1, KEYS), jax.random.fold_in(keys[2], 1), 1, KEYS - 1).astype(jnp.int32)
    value_up = bell_draw(keys[3], (HEADS, LAT, VHEAD), LAT ** -0.5, 0.25, ((0, 8),))
    out_proj = bell_draw(keys[4], (HEADS, VHEAD, D), (HEADS * VHEAD) ** -0.5, 0.09375, ((0, 8),))
    stream = bell_draw(keys[5], (Q_ROWS, D), 1.0, 6.0, ((0, 32),))
    norm_gain = jnp.clip(1.0 + 0.18 * jax.random.normal(keys[6], (D,), jnp.float32), 0.099609375, 1.8984375).astype(jnp.bfloat16)
    expert_ids_keys = jax.random.split(jax.random.fold_in(keys[7], 1), Q_ROWS // Q_DEV)
    expert_ids_turns = jax.random.permutation(jax.random.fold_in(keys[7], 3), Q_ROWS // Q_DEV)
    expert_ids = jax.vmap(lambda own, number: assign_block(jax.random.fold_in(keys[7], 2), own, number, Q_DEV, EXPERTS, TOP, CAP, 2))(expert_ids_keys, expert_ids_turns).reshape((Q_ROWS, TOP))
    gate_weights = jnp.clip(jnp.exp(math.log(0.4) - 2.0794415 * jax.random.uniform(keys[8], (Q_ROWS, TOP), jnp.float32) ** levels(keys[8], (Q_ROWS, TOP), ((0, 32),), -0.2, 0.2)), 0.05, 0.4)
    w_gate = bell_draw(keys[9], (EXPERTS, D, FF), D ** -0.5, 0.125, ((0, 256),))
    w_up = bell_draw(keys[10], (EXPERTS, D, FF), D ** -0.5, 0.125, ((0, 256),))
    w_down = bell_draw(keys[11], (EXPERTS, FF, D), FF ** -0.5, 0.25, ((0, 256),))
    out_grad = bell_draw(keys[12], (Q_ROWS, D), 1.0, 6.0, ((0, 32),))
    return dict(queries=queries, key_latents=key_latents, query_pos=query_pos, value_up=value_up, out_proj=out_proj, stream=stream, norm_gain=norm_gain, expert_ids=expert_ids, gate_weights=gate_weights, w_gate=w_gate, w_up=w_up, w_down=w_down, out_grad=out_grad)


EPSILON = 1e-06

def contract_last(left, right):
    return lax.dot_general(left, right, (((1,), (1,)), ((), ())), preferred_element_type=jnp.float32)

def contract_first(left, right):
    return lax.dot_general(left, right, (((0,), (0,)), ((), ())), preferred_element_type=jnp.float32)

def expert_rows(inputs, upstream, gate_mat, up_mat, down_mat):
    act_gate = jnp.dot(inputs, gate_mat, preferred_element_type=jnp.float32)
    act_up = jnp.dot(inputs, up_mat, preferred_element_type=jnp.float32)
    hidden_back = contract_last(upstream, down_mat)
    sigmoid_g = jax.nn.sigmoid(act_gate)
    gate_back = (hidden_back * act_up * sigmoid_g * (1.0 + act_gate * (1.0 - sigmoid_g))).astype(jnp.bfloat16)
    up_back = (hidden_back * act_gate * sigmoid_g).astype(jnp.bfloat16)
    return (contract_last(gate_back, gate_mat) + contract_last(up_back, up_mat)).astype(jnp.bfloat16)

def reference(queries, key_latents, query_pos, value_up, out_proj, stream, norm_gain, expert_ids, gate_weights, w_gate, w_up, w_down, out_grad):
    stream_f = stream.astype(jnp.float32)
    gain_f = norm_gain.astype(jnp.float32)
    inv_rms = lax.rsqrt(lax.optimization_barrier(jnp.mean(stream_f * stream_f, axis=1, keepdims=True)) + EPSILON)
    normed = (stream_f * inv_rms * gain_f).astype(jnp.bfloat16)
    block_ids = expert_ids.reshape(N_CTX, Q_DEV * TOP)
    onehot = (block_ids[:, :, None] == jnp.arange(EXPERTS, dtype=jnp.int32)[None, None, :]).astype(jnp.int32)
    slot_idx = lax.optimization_barrier(jnp.sum((jnp.cumsum(onehot, axis=1) - 1) * onehot, axis=2)).reshape(Q_ROWS, TOP).astype(jnp.int32)
    block_of = (jnp.arange(Q_ROWS, dtype=jnp.int32) // Q_DEV).astype(jnp.int32)
    place = (block_of[:, None] * CAP + slot_idx).astype(jnp.int32)
    row_ids = jnp.broadcast_to(jnp.arange(Q_ROWS, dtype=jnp.int32)[:, None], (Q_ROWS, TOP))
    slot_table = jnp.full((EXPERTS, N_CTX * CAP), Q_ROWS, jnp.int32).at[expert_ids, place].set(row_ids)
    padded_x = jnp.concatenate([normed, jnp.zeros((1, D), normed.dtype)], axis=0)
    padded_y = jnp.concatenate([out_grad, jnp.zeros((1, D), out_grad.dtype)], axis=0)

    def one_expert(operands):
        table_row, gate_mat, up_mat, down_mat = operands
        return expert_rows(padded_x[table_row], padded_y[table_row], gate_mat, up_mat, down_mat)
    expert_grads = lax.map(one_expert, (slot_table, w_gate, w_up, w_down))
    picked = expert_grads[expert_ids, place]
    normed_grad = lax.optimization_barrier(jnp.sum(gate_weights.astype(jnp.float32)[:, :, None] * picked.astype(jnp.float32), axis=1))
    scaled = normed_grad * gain_f
    branch = inv_rms * scaled - stream_f * inv_rms ** 3 * lax.optimization_barrier(jnp.mean(scaled * stream_f, axis=1, keepdims=True))
    stream_grad = (out_grad.astype(jnp.float32) + branch).astype(jnp.bfloat16)
    head_grad = jnp.einsum('rd,hvd->rhv', stream_grad.astype(jnp.float32), out_proj.astype(jnp.float32), precision=lax.Precision.HIGHEST).astype(jnp.bfloat16)
    latent_grad = jnp.einsum('rhv,hlv->rhl', head_grad.astype(jnp.float32), value_up.astype(jnp.float32), precision=lax.Precision.HIGHEST).astype(jnp.bfloat16)
    scale_q = (VHEAD + ROPE) ** (-0.5)
    visible = jnp.arange(KEYS, dtype=jnp.int32)[None, :] <= query_pos[:, None]
    values = key_latents[:, :LAT]

    def one_head(running, operands):
        query_h, grad_h = operands
        scores = contract_last(query_h, key_latents) * scale_q
        scores = jnp.where(visible, scores, -jnp.inf)
        top_score = lax.optimization_barrier(jnp.max(scores, axis=1, keepdims=True))
        exp_terms = jnp.exp(scores - top_score)
        row_total = lax.optimization_barrier(jnp.sum(exp_terms, axis=1, keepdims=True))
        probs_f = exp_terms / row_total
        probs = probs_f.astype(jnp.bfloat16)
        latent_out = jnp.dot(probs, values, preferred_element_type=jnp.float32)
        delta_row = lax.optimization_barrier(jnp.sum(grad_h.astype(jnp.float32) * latent_out, axis=1, keepdims=True))
        prob_grad = contract_last(grad_h, values)
        score_grad = (probs_f * (prob_grad - delta_row) * scale_q).astype(jnp.bfloat16)
        query_part = jnp.dot(score_grad, key_latents, preferred_element_type=jnp.float32).astype(jnp.bfloat16)
        key_part = contract_first(score_grad, query_h)
        value_part = contract_first(probs, grad_h)
        value_full = jnp.concatenate([value_part, jnp.zeros((KEYS, ROPE), jnp.float32)], axis=1)
        return (running + key_part + value_full, query_part)
    key_sum, query_parts = lax.scan(one_head, jnp.zeros((KEYS, KW), jnp.float32), (jnp.transpose(queries, (1, 0, 2)), jnp.transpose(latent_grad, (1, 0, 2))))
    query_grad = jnp.transpose(query_parts, (1, 0, 2))
    return (stream_grad, query_grad, key_sum.astype(jnp.bfloat16))
```

```python
import functools

import jax
import jax.numpy as jnp
from jax import lax
from jax.experimental import pallas as pl
from jax.experimental.pallas import tpu as pltpu
from jax.sharding import Mesh, PartitionSpec as P

LAT = 512
ROPE = 64
VHEAD = 128
SLOTS = 8
EPSILON = 1e-06
SCALE = (VHEAD + ROPE) ** (-0.5)
BF = jnp.bfloat16
F32 = jnp.float32
CTX = ("y", "x", "zl")
MIB = 1 << 20


def dot(left, right):
    return jnp.dot(left, right, preferred_element_type=F32)


def contract_last(left, right):
    return lax.dot_general(left, right, (((1,), (1,)), ((), ())), preferred_element_type=F32)


def contract_first(left, right):
    return lax.dot_general(left, right, (((0,), (0,)), ((), ())), preferred_element_type=F32)


def call(body, outs, args, vmem_mib, flops=0, scratch=()):
    size = sum(a.size * a.dtype.itemsize for a in args) + sum(
        o.size * jnp.dtype(o.dtype).itemsize for o in outs
    )
    return pl.pallas_call(
        body,
        out_shape=tuple(outs),
        in_specs=[pl.BlockSpec(memory_space=pltpu.SMEM)]
        + [pl.BlockSpec(memory_space=pltpu.VMEM)] * (len(args) - 1),
        out_specs=tuple(pl.BlockSpec(memory_space=pltpu.VMEM) for _ in outs),
        scratch_shapes=list(scratch),
        compiler_params=pltpu.CompilerParams(vmem_limit_bytes=vmem_mib * MIB),
        cost_estimate=pl.CostEstimate(flops=flops, bytes_accessed=size, transcendentals=0),
    )(*args)


def shape(dims, dtype):
    return jax.ShapeDtypeStruct(dims, dtype)


def prep_kernel(exp_count, pos, ids, gates, stream, gain, out_grad, send, weight):
    rows, width = stream.shape
    slots = weight.shape[0]
    place = lax.broadcasted_iota(jnp.int32, (slots, rows), 0)
    expert = (place // SLOTS) * exp_count + pos[0]
    member = jnp.zeros((slots, rows), F32)
    weighting = jnp.zeros((slots, rows), F32)
    for k in range(ids.shape[0]):
        hit = ids[k : k + 1, :] == expert
        member = jnp.where(hit, 1.0, member)
        weighting = jnp.where(hit, gates[k : k + 1, :], weighting)
    before = (
        lax.broadcasted_iota(jnp.int32, (rows, rows), 0)
        < lax.broadcasted_iota(jnp.int32, (rows, rows), 1)
    ).astype(F32).astype(BF)
    rank = dot(member.astype(BF), before)
    chosen = (member > 0.5) & (rank == (place % SLOTS).astype(F32))
    select = jnp.where(chosen, 1.0, 0.0).astype(BF)
    weight[...] = jnp.where(chosen, weighting, 0.0)
    step = width // 3
    for c in range(0, width, step):
        send[:, width + c : width + c + step] = dot(select, out_grad[:, c : c + step]).astype(BF)
    stream_f = stream[...].astype(F32)
    inv_rms = lax.rsqrt(jnp.mean(stream_f * stream_f, axis=1, keepdims=True) + EPSILON)
    normed = (stream_f * inv_rms * gain[...].astype(F32)).astype(BF)
    for c in range(0, width, step):
        send[:, c : c + step] = dot(select, normed[:, c : c + step]).astype(BF)


def expert_kernel(pos, rows, w_gate, w_up, w_down, grads):
    width = w_gate.shape[0]
    act_gate = dot(rows[:, :width], w_gate[...])
    act_up = dot(rows[:, :width], w_up[...])
    hidden_back = contract_last(rows[:, width:], w_down[...])
    sig = jax.nn.sigmoid(act_gate)
    gate_back = (hidden_back * act_up * sig * (1.0 + act_gate * (1.0 - sig))).astype(BF)
    up_back = (hidden_back * act_gate * sig).astype(BF)
    step = width // 3
    for c in range(0, width, step):
        grads[:, c : c + step] = (
            contract_last(gate_back, w_gate[c : c + step, :])
            + contract_last(up_back, w_up[c : c + step, :])
        ).astype(BF)


def combine_kernel(pos, returned, weight, keep, send, total):
    half = keep.shape[0]
    w = weight[...]
    high = w.astype(BF)
    low = (w - high.astype(F32)).astype(BF)
    both = jnp.concatenate([high, low], axis=0)
    width = returned.shape[1]
    step = width // 3
    for c in range(0, width, step):
        part = returned[:, c : c + step]
        total[:, c : c + step] = contract_first(both, jnp.concatenate([part, part], axis=0))
    keep[...] = total[pl.ds(pl.multiple_of(pos[1] * half, half), half), :]
    send[...] = total[pl.ds(pl.multiple_of((1 - pos[1]) * half, half), half), :].astype(BF)


def pair_kernel(pos, keep, received, own, *sends):
    total = keep[...] + received[...].astype(F32)
    keep_rows = own.shape[0]
    count = len(sends) + 1
    for place in range(count):
        rows = total[place * keep_rows : (place + 1) * keep_rows, :]

        def put(rows=rows, place=place):
            @pl.when(pos[2] == place)
            def _():
                own[...] = rows

            for s, send in enumerate(sends):

                @pl.when(lax.rem(pos[2] + s + 1, count) == place)
                def _(send=send):
                    send[...] = rows.astype(BF)

        put()


def stream_kernel(pos, own, got_1, got_2, got_3, stream, gain, out_grad, stream_grad):
    rows = own.shape[0]
    normed_grad = (
        own[...] + got_1[...].astype(F32) + got_2[...].astype(F32) + got_3[...].astype(F32)
    )
    here = pl.ds(pl.multiple_of((pos[1] * 4 + pos[2]) * rows, rows), rows)
    stream_f = stream[here, :].astype(F32)
    gain_f = gain[...].astype(F32)
    inv_rms = lax.rsqrt(jnp.mean(stream_f * stream_f, axis=1, keepdims=True) + EPSILON)
    scaled = normed_grad * gain_f
    branch = inv_rms * scaled - stream_f * (inv_rms * inv_rms * inv_rms) * jnp.mean(
        scaled * stream_f, axis=1, keepdims=True
    )
    stream_grad[...] = (out_grad[here, :].astype(F32) + branch).astype(BF)


def latent_kernel(pos, *refs):
    pieces, (out_proj, value_up, latent_out), (stream_grad, latent_t, latent_rows, delta) = (
        refs[:8],
        refs[8:11],
        refs[11:],
    )
    rows = pieces[0].shape[0]
    for side in range(2):
        core = pos[1] if side == 0 else 1 - pos[1]
        for s in range(4):
            place = core * 4 + lax.rem(pos[2] - s + 4, 4)
            here = pl.ds(pl.multiple_of(place * rows, rows), rows)
            stream_grad[here, :] = pieces[side * 4 + s][...]
    heads, lat, vhead = value_up.shape
    count = stream_grad.shape[0]
    all_rows = stream_grad[...]
    for h in range(heads):
        head_t = contract_last(out_proj[h], all_rows).astype(BF)
        grad_t = dot(value_up[h], head_t).astype(BF)
        cols = slice(h * count, (h + 1) * count)
        latent_t[:, cols] = grad_t
        grad_f = grad_t.astype(F32)
        delta[:, cols] = jnp.sum(grad_f * latent_out[:, cols], axis=0, keepdims=True)
        latent_rows[cols, :] = grad_f.T.astype(BF)


def scores_kernel(
    key_block, pos, mine, other, queries_t, seen, prob_mine, prob_other, latent_out, query_rows, scratch
):
    heads, width, rows = queries_t.shape
    half = mine.shape[0]
    chunk = 256
    for h in range(heads):
        query_rows[h * rows : (h + 1) * rows, :] = queries_t[h].astype(F32).T.astype(BF)
    for pair in range(heads // 2):
        query = jnp.concatenate([queries_t[2 * pair], queries_t[2 * pair + 1]], axis=1)
        last = jnp.concatenate([seen[...], seen[...]], axis=1)
        cols = slice(2 * pair * rows, 2 * (pair + 1) * rows)
        top = jnp.full((1, 2 * rows), -jnp.inf, F32)
        for side, keys in enumerate((mine, other)):
            core = pos[1] if side == 0 else 1 - pos[1]

            def score(c, top, side=side, keys=keys, core=core):
                at = pl.multiple_of(c * chunk, chunk)
                s = dot(keys[pl.ds(at, chunk), :], query) * SCALE
                index = lax.broadcasted_iota(jnp.int32, (chunk, 2 * rows), 0) + at
                key = (index // key_block) * (2 * key_block) + core * key_block + index % key_block
                s = jnp.where(key <= last, s, -jnp.inf)
                scratch[pl.ds(side * half + at, chunk), :] = s
                return jnp.maximum(top, jnp.max(s, axis=0, keepdims=True))

            top = lax.fori_loop(0, half // chunk, score, top)

        def expo(c, total):
            here = pl.ds(pl.multiple_of(c * chunk, chunk), chunk)
            e = jnp.exp(scratch[here, :] - top)
            scratch[here, :] = e
            return total + jnp.sum(e, axis=0, keepdims=True)

        total = lax.fori_loop(0, 2 * half // chunk, expo, jnp.zeros((1, 2 * rows), F32))
        inverse = 1.0 / total
        latent_out[:, cols] = jnp.zeros((LAT, 2 * rows), F32)
        for side, (keys, probs) in enumerate(((mine, prob_mine), (other, prob_other))):

            def finish(c, carry, side=side, keys=keys, probs=probs):
                at = pl.multiple_of(c * chunk, chunk)
                p = (scratch[pl.ds(side * half + at, chunk), :] * inverse).astype(BF)
                probs[pl.ds(at, chunk), cols] = p
                latent_out[:, cols] += contract_first(keys[pl.ds(at, chunk), :LAT], p)
                return carry

            lax.fori_loop(0, half // chunk, finish, 0)


def back_kernel(pos, keys, probs, latent_t, latent_rows, delta, query_rows, score_grad, key_grad):
    chunk = 256

    def step(c, carry):
        here = pl.ds(pl.multiple_of(c * chunk, chunk), chunk)
        p = probs[here, :]
        prob_grad = dot(keys[here, :LAT], latent_t[...])
        sg = (p.astype(F32) * (prob_grad - delta[...]) * SCALE).astype(BF)
        score_grad[here, :] = sg
        key_part = dot(sg, query_rows[...])
        value_part = dot(p, latent_rows[...])
        key_grad[here, :LAT] = (key_part[:, :LAT] + value_part).astype(BF)
        key_grad[here, LAT:] = key_part[:, LAT:].astype(BF)
        return carry

    lax.fori_loop(0, keys.shape[0] // chunk, step, 0)


def query_kernel(pos, mine, other, grad_mine, grad_other, out):
    heads, _, rows = out.shape
    for pair in range(heads // 2):
        cols = slice(2 * pair * rows, 2 * (pair + 1) * rows)
        total = contract_first(mine[...], grad_mine[:, cols]) + contract_first(
            other[...], grad_other[:, cols]
        )
        for i in range(2):
            out[2 * pair + i] = total[:, i * rows : (i + 1) * rows].astype(BF)


def final_kernel(pos, own, got_1, got_2, got_3, out, slots):
    slots[pos[2]] = own[...].astype(F32)
    for s, got in enumerate((got_1, got_2, got_3)):
        slots[lax.rem(pos[2] + 4 - (s + 1), 4)] = got[...].astype(F32)
    out[...] = (slots[0] + slots[1] + slots[2] + slots[3]).astype(BF)


def swap(value):
    return lax.ppermute(value, "co", [(0, 1), (1, 0)])


def turn(value, shift):
    return lax.ppermute(value, "zh", [(i, (i + shift) % 4) for i in range(4)])


def exchange(value):
    return lax.all_to_all(value, CTX, split_axis=0, concat_axis=0, tiled=True)


def shards(
    queries,
    key_latents,
    query_pos,
    value_up,
    out_proj,
    stream,
    norm_gain,
    expert_ids,
    gate_weights,
    w_gate,
    w_up,
    w_down,
    out_grad,
):
    ctx_count = lax.axis_size(CTX)
    exp_count = lax.axis_size("zh") * lax.axis_size("co")
    rows, width = stream.shape
    slots = ctx_count * SLOTS
    core = lax.axis_index("co")
    group = lax.axis_index("zh")
    pos = jnp.stack([group * 2 + core, core, group]).astype(jnp.int32)
    gain = norm_gain.reshape(1, width)
    hidden = w_gate.shape[2]

    send, weight = call(
        functools.partial(prep_kernel, exp_count),
        [shape((slots, 2 * width), BF), shape((slots, rows), F32)],
        [pos, expert_ids.T, gate_weights.T, stream, gain, out_grad],
        24,
        flops=4 * slots * rows * width,
    )
    arrived = exchange(send.reshape(ctx_count, SLOTS, 2 * width)).reshape(slots, 2 * width)
    (grads,) = call(
        expert_kernel,
        [shape((slots, width), BF)],
        [pos, arrived, w_gate[0], w_up[0], w_down[0]],
        32,
        flops=10 * slots * width * hidden,
    )
    returned = exchange(grads.reshape(ctx_count, SLOTS, width)).reshape(slots, width)

    half_keys = key_latents.shape[0] // 2
    key_half = lax.dynamic_slice_in_dim(key_latents, core * half_keys, half_keys, 0)
    key_send = jnp.broadcast_to(key_half[None], (ctx_count,) + key_half.shape)
    key_send, returned = lax.optimization_barrier((key_send, returned))

    keep, other_part = call(
        combine_kernel,
        [shape((rows // 2, width), F32), shape((rows // 2, width), BF)],
        [pos, returned, weight],
        24,
        flops=8 * slots * rows * width,
        scratch=[pltpu.VMEM((rows, width), F32)],
    )
    received = swap(other_part)
    piece = rows // 8
    own, *sends = call(
        pair_kernel,
        [shape((piece, width), F32)] + [shape((piece, width), BF)] * 3,
        [pos, keep, received],
        16,
    )
    got = [turn(value, s + 1) for s, value in enumerate(sends)]
    (piece_grad,) = call(
        stream_kernel,
        [shape((piece, width), BF)],
        [pos, own, *got, stream, gain, out_grad],
        16,
    )
    pieces = [piece_grad] + [turn(piece_grad, s + 1) for s in range(3)]
    pieces = pieces + [swap(value) for value in pieces]

    mine = exchange(key_send).reshape(ctx_count * half_keys, -1)
    other = swap(mine)
    key_width = key_latents.shape[1]
    half = ctx_count * half_keys
    heads = queries.shape[1]
    flat = heads * rows
    queries_t = jnp.transpose(queries, (1, 2, 0))
    prob_mine, prob_other, latent_out, query_rows = call(
        functools.partial(scores_kernel, half_keys),
        [
            shape((half, flat), BF),
            shape((half, flat), BF),
            shape((LAT, flat), F32),
            shape((flat, key_width), BF),
        ],
        [pos, mine, other, queries_t, query_pos.reshape(1, rows)],
        32,
        flops=4 * half * flat * (key_width + LAT),
        scratch=[pltpu.VMEM((2 * half, 2 * rows), F32)],
    )

    stream_grad, latent_t, latent_rows, delta = call(
        latent_kernel,
        [
            shape((rows, width), BF),
            shape((LAT, flat), BF),
            shape((flat, LAT), BF),
            shape((1, flat), F32),
        ],
        [pos, *pieces, out_proj, value_up, latent_out],
        24,
        flops=2 * flat * VHEAD * (width + LAT),
    )

    def back(keys, probs):
        return call(
            back_kernel,
            [shape((half, flat), BF), shape((half, key_width), BF)],
            [pos, keys, probs, latent_t, latent_rows, delta, query_rows],
            24,
            flops=2 * half * flat * (2 * LAT + key_width),
        )

    grad_other, key_other = back(other, prob_other)
    key_received = swap(key_other)
    grad_mine, key_mine = back(mine, prob_mine)
    key_sum = (key_mine.astype(F32) + key_received.astype(F32)).astype(BF)
    key_parts = exchange(key_sum.reshape(ctx_count, half_keys, key_width))
    (query_grad_t,) = call(
        query_kernel,
        [shape((heads, key_width, rows), BF)],
        [pos, mine, other, grad_mine, grad_other],
        24,
        flops=4 * half * flat * key_width,
    )
    query_grad = jnp.transpose(query_grad_t, (2, 0, 1))
    key_own = jnp.sum(key_parts.astype(F32), axis=0).astype(BF)
    (key_final,) = call(
        final_kernel,
        [shape((half_keys, key_width), BF)],
        [pos, key_own, *[turn(key_own, s + 1) for s in range(3)]],
        16,
        scratch=[pltpu.VMEM((4, half_keys, key_width), F32)],
    )
    key_pair = swap(key_final)
    key_grad = jnp.where(
        core == 0,
        jnp.concatenate([key_final, key_pair], axis=0),
        jnp.concatenate([key_pair, key_final], axis=0),
    )
    return (stream_grad, query_grad, key_grad)


def solution(mesh):
    fine = Mesh(mesh.devices.reshape(4, 4, 2, 4, 2), ("y", "x", "zl", "zh", "co"))
    exp = ("zh", "co")
    both = CTX + exp
    placed = (
        P(CTX, exp, None),
        P(CTX, None),
        P(CTX),
        P(exp, None, None),
        P(exp, None, None),
        P(CTX, None),
        P(),
        P(CTX, None),
        P(CTX, None),
        P(both, None, None),
        P(both, None, None),
        P(both, None, None),
        P(CTX, None),
    )
    return jax.shard_map(
        shards,
        mesh=fine,
        in_specs=placed,
        out_specs=(P(CTX, None), P(CTX, exp, None), P(CTX, None)),
        check_vma=False,
    )
```

```python
import functools

import jax
import jax.numpy as jnp
from jax import lax
from jax.experimental import pallas as pl
from jax.experimental.pallas import tpu as pltpu
from jax.sharding import Mesh, PartitionSpec as P

LAT = 512
ROPE = 64
VHEAD = 128
PACK = 4
SLOTS = 8
TOP = 8
EPSILON = 1e-06
SCALE = (VHEAD + ROPE) ** (-0.5)
BF = jnp.bfloat16
F32 = jnp.float32
CTX = ("y", "x", "zl")
EXP = ("zh", "co")
MIB = 1 << 20


def dot(left, right):
    return jnp.dot(left, right, preferred_element_type=F32)


def contract_last(left, right):
    return lax.dot_general(left, right, (((1,), (1,)), ((), ())), preferred_element_type=F32)


def contract_first(left, right):
    return lax.dot_general(left, right, (((0,), (0,)), ((), ())), preferred_element_type=F32)


def call(body, outs, args, vmem_mib, flops=0, scratch=(), far=(), far_out=()):
    size = sum(a.size * a.dtype.itemsize for a in args) + sum(
        o.size * jnp.dtype(o.dtype).itemsize for o in outs
    )

    def place(away):
        return pl.BlockSpec(memory_space=pltpu.HBM if away else pltpu.VMEM)

    return pl.pallas_call(
        body,
        out_shape=tuple(outs),
        in_specs=[pl.BlockSpec(memory_space=pltpu.SMEM)]
        + [place(i in far) for i in range(1, len(args))],
        out_specs=tuple(place(i in far_out) for i in range(len(outs))),
        scratch_shapes=list(scratch),
        compiler_params=pltpu.CompilerParams(vmem_limit_bytes=vmem_mib * MIB),
        cost_estimate=pl.CostEstimate(flops=flops, bytes_accessed=size, transcendentals=0),
    )(*args)


def shape(dims, dtype):
    return jax.ShapeDtypeStruct(dims, dtype)


def prep_kernel(exp_count, pos, *refs):
    far, (send, weight), held, arrived = refs[:6], refs[6:8], refs[8:14], refs[14]
    copies = [
        pltpu.make_async_copy(source, target, arrived.at[i])
        for i, (source, target) in enumerate(zip(far, held))
    ]
    for copy in copies:
        copy.start()
    ids, gates, stream, gain, out_grad, keys = held
    copies[0].wait()
    copies[1].wait()
    rows, width = stream.shape
    slots = weight.shape[0]
    place = lax.broadcasted_iota(jnp.int32, (slots, rows), 0)
    expert = (place // SLOTS) * exp_count + pos[0]
    member = jnp.zeros((slots, rows), F32)
    weighting = jnp.zeros((slots, rows), F32)
    for k in range(ids.shape[0]):
        hit = ids[k : k + 1, :] == expert
        member = jnp.where(hit, 1.0, member)
        weighting = jnp.where(hit, gates[k : k + 1, :], weighting)
    before = (
        lax.broadcasted_iota(jnp.int32, (rows, rows), 0)
        < lax.broadcasted_iota(jnp.int32, (rows, rows), 1)
    ).astype(F32).astype(BF)
    rank = dot(member.astype(BF), before)
    chosen = (member > 0.5) & (rank == (place % SLOTS).astype(F32))
    select = jnp.where(chosen, 1.0, 0.0).astype(BF)
    weight[...] = jnp.where(chosen, weighting, 0.0)
    step = width // 3
    copies[4].wait()
    for c in range(0, width, step):
        send[:, width + c : width + c + step] = dot(select, out_grad[:, c : c + step]).astype(BF)
    copies[2].wait()
    copies[3].wait()
    stream_f = stream[...].astype(F32)
    inv_rms = lax.rsqrt(jnp.mean(stream_f * stream_f, axis=1, keepdims=True) + EPSILON)
    normed = (stream_f * inv_rms * gain[...].astype(F32)).astype(BF)
    for c in range(0, width, step):
        send[:, c : c + step] = dot(select, normed[:, c : c + step]).astype(BF)
    copies[5].wait()
    count = keys.shape[0]
    row = lax.broadcasted_iota(jnp.int32, (slots, count), 0) % SLOTS
    key = lax.broadcasted_iota(jnp.int32, (slots, count), 1)
    ropes = []
    for q in range(PACK):
        wanted = pos[1] * (count // 2) + q * SLOTS + row
        pick = jnp.where(key == wanted, 1.0, 0.0).astype(BF)
        at = 2 * width + q * LAT
        send[:, at : at + LAT] = dot(pick, keys[:, :LAT]).astype(BF)
        ropes.append(dot(pick, keys[:, LAT:]))
    send[:, 2 * width + PACK * LAT :] = jnp.concatenate(ropes, axis=1).astype(BF)


def expert_kernel(pos, rows, w_gate, w_up, w_down_far, grads, key_pack, w_down, arrived):
    width = w_gate.shape[0]
    load = pltpu.make_async_copy(w_down_far, w_down, arrived.at[0])
    load.start()
    store = pltpu.make_async_copy(rows.at[:, 2 * width :], key_pack, arrived.at[1])
    store.start()
    act_gate = dot(rows[:, :width], w_gate[...])
    act_up = dot(rows[:, :width], w_up[...])
    load.wait()
    hidden_back = contract_last(rows[:, width : 2 * width], w_down[...])
    sig = jax.nn.sigmoid(act_gate)
    gate_back = (hidden_back * act_up * sig * (1.0 + act_gate * (1.0 - sig))).astype(BF)
    up_back = (hidden_back * act_gate * sig).astype(BF)
    step = width // 3
    for c in range(0, width, step):
        grads[:, c : c + step] = (
            contract_last(gate_back, w_gate[c : c + step, :])
            + contract_last(up_back, w_up[c : c + step, :])
        ).astype(BF)
    store.wait()


def combine_kernel(pos, returned, weight, keep, send, total):
    half = keep.shape[0]
    w = weight[...]
    high = w.astype(BF)
    low = (w - high.astype(F32)).astype(BF)
    both = jnp.concatenate([high, low], axis=0)
    width = returned.shape[1]
    step = width // 3
    for c in range(0, width, step):
        part = returned[:, c : c + step]
        total[:, c : c + step] = contract_first(both, jnp.concatenate([part, part], axis=0))
    piece = half // 4
    for z in range(4):
        here = slice(z * piece, (z + 1) * piece)
        first = pl.multiple_of((2 * z + pos[1]) * piece, piece)
        second = pl.multiple_of((2 * z + 1 - pos[1]) * piece, piece)
        keep[here, :] = total[pl.ds(first, piece), :]
        send[here, :] = total[pl.ds(second, piece), :].astype(BF)


def pair_kernel(pos, keep, received, own, *sends):
    total = keep[...] + received[...].astype(F32)
    keep_rows = own.shape[0]
    count = len(sends) + 1
    for place in range(count):
        rows = total[place * keep_rows : (place + 1) * keep_rows, :]

        def put(rows=rows, place=place):
            @pl.when(pos[2] == place)
            def _():
                own[...] = rows

            for s, send in enumerate(sends):

                @pl.when(lax.rem(pos[2] + s + 1, count) == place)
                def _(send=send):
                    send[...] = rows.astype(BF)

        put()


def stream_kernel(pos, own, got_1, got_2, got_3, stream, gain, out_grad, stream_grad):
    rows = own.shape[0]
    normed_grad = (
        own[...] + got_1[...].astype(F32) + got_2[...].astype(F32) + got_3[...].astype(F32)
    )
    here = pl.ds(pl.multiple_of(pos[0] * rows, rows), rows)
    stream_f = stream[here, :].astype(F32)
    gain_f = gain[...].astype(F32)
    inv_rms = lax.rsqrt(jnp.mean(stream_f * stream_f, axis=1, keepdims=True) + EPSILON)
    scaled = normed_grad * gain_f
    branch = inv_rms * scaled - stream_f * (inv_rms * inv_rms * inv_rms) * jnp.mean(
        scaled * stream_f, axis=1, keepdims=True
    )
    stream_grad[...] = (out_grad[here, :].astype(F32) + branch).astype(BF)


def latent_kernel(
    pos, stream_grad, out_proj, value_up, latent_out, latent_t, latent_rows, delta
):
    heads, lat, vhead = value_up.shape
    count = stream_grad.shape[0]
    all_rows = stream_grad[...]
    for h in range(heads):
        head_t = contract_last(out_proj[h], all_rows).astype(BF)
        grad_t = dot(value_up[h], head_t).astype(BF)
        cols = slice(h * count, (h + 1) * count)
        latent_t[:, cols] = grad_t
        grad_f = grad_t.astype(F32)
        delta[:, cols] = jnp.sum(grad_f * latent_out[:, cols], axis=0, keepdims=True)
        latent_rows[cols, :] = grad_f.T.astype(BF)


def rope_lanes(q):
    at = PACK * LAT + (q // 2) * 2 * ROPE
    return slice(at, at + 2 * ROPE)


def scores_kernel(
    pos,
    mine_far,
    other_far,
    queries_t,
    seen,
    probs_far,
    latent_far,
    rows_far,
    mine,
    other,
    scratch,
    probs,
    latent_out,
    query_rows,
    arrived,
):
    heads, width, rows = queries_t.shape
    slots = mine.shape[0]
    count = heads * rows
    loads = [
        pltpu.make_async_copy(mine_far, mine, arrived.at[0]),
        pltpu.make_async_copy(other_far, other, arrived.at[1]),
    ]
    for load in loads:
        load.start()
    blank = jnp.zeros((ROPE, count), BF)
    query = jnp.concatenate([queries_t[h] for h in range(heads)], axis=1)
    rope = query[LAT:, :]
    ropes = [jnp.concatenate([rope, blank], axis=0), jnp.concatenate([blank, rope], axis=0)]
    stacked = jnp.concatenate([query[:LAT, :]] + ropes, axis=0)
    query_rows[...] = stacked.astype(F32).T.astype(BF)
    stores = [pltpu.make_async_copy(query_rows, rows_far, arrived.at[2])]
    stores[0].start()
    last = jnp.concatenate([seen[...]] * heads, axis=1)
    place = lax.broadcasted_iota(jnp.int32, (slots, 1), 0)
    slot_key = (place // SLOTS) * (2 * PACK * SLOTS) + place % SLOTS
    top = jnp.full((1, count), -jnp.inf, F32)
    for side, keys in enumerate((mine, other)):
        loads[side].wait()
        core = pos[1] if side == 0 else 1 - pos[1]
        for q in range(PACK):
            s = dot(keys[:, q * LAT : (q + 1) * LAT], query[:LAT, :])
            s = (s + dot(keys[:, rope_lanes(q)], ropes[q % 2])) * SCALE
            key = slot_key + (core * (PACK * SLOTS) + q * SLOTS)
            s = jnp.where(key <= last, s, -jnp.inf)
            scratch[side * PACK + q] = s
            top = jnp.maximum(top, jnp.max(s, axis=0, keepdims=True))
    total = jnp.zeros((1, count), F32)
    for c in range(2 * PACK):
        e = jnp.exp(scratch[c] - top)
        scratch[c] = e
        total = total + jnp.sum(e, axis=0, keepdims=True)
    inverse = 1.0 / total
    for c in range(2 * PACK):
        q = c % PACK
        p = (scratch[c] * inverse).astype(BF)
        probs[c] = p
        store = pltpu.make_async_copy(probs.at[c], probs_far.at[c], arrived.at[3 + c])
        store.start()
        stores.append(store)
        part = contract_first((mine if c < PACK else other)[:, q * LAT : (q + 1) * LAT], p)
        if c == 0:
            latent_out[...] = part
        else:
            latent_out[...] += part
    store = pltpu.make_async_copy(latent_out, latent_far, arrived.at[3 + 2 * PACK])
    store.start()
    for store in stores + [store]:
        store.wait()


def back_kernel(
    side, pos, keys, probs, latent_t, latent_rows, delta, query_rows, key_grad, score_far, score_grad, sent
):
    stores = []
    part = []
    for q in range(PACK):
        p = probs[side * PACK + q]
        lanes = slice(q * LAT, (q + 1) * LAT)
        prob_grad = dot(keys[:, lanes], latent_t[...])
        sg = (p.astype(F32) * (prob_grad - delta[...]) * SCALE).astype(BF)
        score_grad[q] = sg
        store = pltpu.make_async_copy(score_grad.at[q], score_far.at[q], sent.at[q])
        store.start()
        stores.append(store)
        key_grad[:, lanes] = (dot(sg, query_rows[:, :LAT]) + dot(p, latent_rows[...])).astype(BF)
        at = LAT + (q % 2) * 2 * ROPE
        part.append(dot(sg, query_rows[:, at : at + 2 * ROPE]))
        if q % 2:
            key_grad[:, rope_lanes(q)] = (part[q - 1] + part[q]).astype(BF)
    for store in stores:
        store.wait()


def query_kernel(pos, *refs):
    far, out, held, arrived = refs[:4], refs[4], refs[5:9], refs[9]
    loads = [
        pltpu.make_async_copy(source, target, arrived.at[i])
        for i, (source, target) in enumerate(zip(far, held))
    ]
    for load in loads:
        load.start()
    for load in loads:
        load.wait()
    heads, width, rows = out.shape
    for pair in range(heads // 2):
        cols = slice(2 * pair * rows, 2 * (pair + 1) * rows)
        total = rope = None
        for keys, grads in ((held[0], held[2]), (held[1], held[3])):
            for q in range(PACK):
                sg = grads[q, :, cols]
                lat_part = contract_first(keys[:, q * LAT : (q + 1) * LAT], sg)
                rope_part = contract_first(keys[:, rope_lanes(q)], sg)
                rope_part = rope_part[(q % 2) * ROPE : (q % 2 + 1) * ROPE, :]
                total = lat_part if total is None else total + lat_part
                rope = rope_part if rope is None else rope + rope_part
        for i in range(2):
            own = slice(i * rows, (i + 1) * rows)
            out[2 * pair + i] = jnp.concatenate([total[:, own], rope[:, own]], axis=0).astype(BF)


def add_kernel(pos, left, right, out):
    out[...] = (left[...].astype(F32) + right[...].astype(F32)).astype(BF)


def sum_kernel(pos, parts, out):
    count, width = parts.shape
    spread = parts[...].astype(F32).reshape(count // SLOTS, SLOTS, width)
    out[...] = jnp.sum(spread, axis=0).astype(BF)


def final_kernel(pos, parts, out):
    spread = parts[...].astype(F32)
    rows = []
    for core in range(2):
        total = None
        for z in range(4):
            at = (2 * z + core) * SLOTS
            part = spread[at : at + SLOTS, :]
            total = part if total is None else total + part
        for q in range(PACK):
            at = PACK * LAT + q * ROPE
            rows.append(
                jnp.concatenate([total[:, q * LAT : (q + 1) * LAT], total[:, at : at + ROPE]], axis=1)
            )
    out[...] = jnp.concatenate(rows, axis=0).astype(BF)


def swap(value):
    return lax.ppermute(value, "co", [(0, 1), (1, 0)])


def turn(value, shift):
    return lax.ppermute(value, "zh", [(i, (i + shift) % 4) for i in range(4)])


def exchange(value):
    return lax.all_to_all(value, CTX, split_axis=0, concat_axis=0, tiled=True)


def shards(
    queries,
    key_latents,
    query_pos,
    value_up,
    out_proj,
    stream,
    norm_gain,
    expert_ids,
    gate_weights,
    w_gate,
    w_up,
    w_down,
    out_grad,
):
    ctx_count = lax.axis_size(CTX)
    exp_count = lax.axis_size("zh") * lax.axis_size("co")
    rows, width = stream.shape
    slots = ctx_count * SLOTS
    core = lax.axis_index("co")
    group = lax.axis_index("zh")
    pos = jnp.stack([group * 2 + core, core, group]).astype(jnp.int32)
    gain = norm_gain.reshape(1, width)
    hidden = w_gate.shape[2]

    key_count, key_width = key_latents.shape
    send, weight = call(
        functools.partial(prep_kernel, exp_count),
        [shape((slots, 3 * width), BF), shape((slots, rows), F32)],
        [pos, expert_ids.T, gate_weights.T, stream, gain, out_grad, key_latents],
        16,
        flops=4 * slots * rows * width,
        scratch=[
            pltpu.VMEM((TOP, rows), jnp.int32),
            pltpu.VMEM((TOP, rows), F32),
            pltpu.VMEM((rows, width), BF),
            pltpu.VMEM((1, width), BF),
            pltpu.VMEM((rows, width), BF),
            pltpu.VMEM((key_count, key_width), BF),
            pltpu.SemaphoreType.DMA((6,)),
        ],
        far=range(1, 7),
    )
    arrived = exchange(send.reshape(ctx_count, SLOTS, 3 * width)).reshape(slots, 3 * width)
    grads, mine = call(
        expert_kernel,
        [shape((slots, width), BF), shape((slots, width), BF)],
        [pos, arrived, w_gate[0], w_up[0], w_down[0]],
        12,
        flops=10 * slots * width * hidden,
        scratch=[pltpu.VMEM((hidden, width), BF), pltpu.SemaphoreType.DMA((2,))],
        far=(4,),
        far_out=(1,),
    )
    returned = exchange(grads.reshape(ctx_count, SLOTS, width))
    other = swap(mine)
    heads = queries.shape[1]
    flat = heads * rows
    half = slots * PACK
    wide = LAT + 4 * ROPE
    probs, latent_out, query_rows = call(
        scores_kernel,
        [
            shape((2 * PACK, slots, flat), BF),
            shape((LAT, flat), F32),
            shape((flat, wide), BF),
        ],
        [pos, mine, other, jnp.transpose(queries, (1, 2, 0)), query_pos.reshape(1, rows)],
        24,
        flops=4 * half * flat * (key_width + LAT),
        scratch=[
            pltpu.VMEM((slots, width), BF),
            pltpu.VMEM((slots, width), BF),
            pltpu.VMEM((2 * PACK, slots, flat), F32),
            pltpu.VMEM((2 * PACK, slots, flat), BF),
            pltpu.VMEM((LAT, flat), F32),
            pltpu.VMEM((flat, wide), BF),
            pltpu.SemaphoreType.DMA((4 + 2 * PACK,)),
        ],
        far=(1, 2),
        far_out=(0, 1, 2),
    )
    returned, probs, latent_out, query_rows = lax.optimization_barrier(
        (returned, probs, latent_out, query_rows)
    )
    returned = returned.reshape(slots, width)

    keep, other_part = call(
        combine_kernel,
        [shape((rows // 2, width), F32), shape((rows // 2, width), BF)],
        [pos, returned, weight],
        8,
        flops=8 * slots * rows * width,
        scratch=[pltpu.VMEM((rows, width), F32)],
    )
    received = swap(other_part)
    piece = rows // 8
    own, *sends = call(
        pair_kernel,
        [shape((piece, width), F32)] + [shape((piece, width), BF)] * 3,
        [pos, keep, received],
        4,
    )
    got = [turn(value, s + 1) for s, value in enumerate(sends)]
    (piece_grad,) = call(
        stream_kernel,
        [shape((piece, width), BF)],
        [pos, own, *got, stream, gain, out_grad],
        4,
    )
    stream_grad = lax.all_gather(piece_grad, EXP, axis=0, tiled=True)


    latent_t, latent_rows, delta = call(
        latent_kernel,
        [
            shape((LAT, flat), BF),
            shape((flat, LAT), BF),
            shape((1, flat), F32),
        ],
        [pos, stream_grad, out_proj, value_up, latent_out],
        8,
        flops=2 * flat * VHEAD * (width + LAT),
    )

    def back(side, keys):
        return call(
            functools.partial(back_kernel, side),
            [shape((slots, width), BF), shape((PACK, slots, flat), BF)],
            [pos, keys, probs, latent_t, latent_rows, delta, query_rows],
            8,
            flops=2 * half * flat * (2 * LAT + key_width),
            scratch=[
                pltpu.VMEM((PACK, slots, flat), BF),
                pltpu.SemaphoreType.DMA((PACK,)),
            ],
            far_out=(1,),
        )

    key_other, grad_other = back(1, other)
    key_received = swap(key_other)
    key_mine, grad_mine = back(0, mine)
    (key_sum,) = call(add_kernel, [shape((slots, width), BF)], [pos, key_mine, key_received], 4)
    key_parts = exchange(key_sum.reshape(ctx_count, SLOTS, width))
    (query_grad_t,) = call(
        query_kernel,
        [shape((heads, key_width, rows), BF)],
        [pos, mine, other, grad_mine, grad_other],
        16,
        flops=4 * half * flat * key_width,
        scratch=[
            pltpu.VMEM((slots, width), BF),
            pltpu.VMEM((slots, width), BF),
            pltpu.VMEM((PACK, slots, flat), BF),
            pltpu.VMEM((PACK, slots, flat), BF),
            pltpu.SemaphoreType.DMA((4,)),
        ],
        far=(1, 2, 3, 4),
    )
    key_parts, query_grad_t = lax.optimization_barrier((key_parts, query_grad_t))
    query_grad = jnp.transpose(query_grad_t, (2, 0, 1))
    (key_own,) = call(
        sum_kernel, [shape((SLOTS, width), BF)], [pos, key_parts.reshape(slots, width)], 8
    )
    (key_grad,) = call(
        final_kernel,
        [shape((key_count, key_width), BF)],
        [pos, lax.all_gather(key_own, EXP, axis=0, tiled=True)],
        4,
    )
    return (stream_grad, query_grad, key_grad)


def solution(mesh):
    fine = Mesh(mesh.devices.reshape(4, 4, 2, 4, 2), ("y", "x", "zl", "zh", "co"))
    exp = EXP
    both = CTX + exp
    placed = (
        P(CTX, exp, None),
        P(CTX, None),
        P(CTX),
        P(exp, None, None),
        P(exp, None, None),
        P(CTX, None),
        P(),
        P(CTX, None),
        P(CTX, None),
        P(both, None, None),
        P(both, None, None),
        P(both, None, None),
        P(CTX, None),
    )
    return jax.shard_map(
        shards,
        mesh=fine,
        in_specs=placed,
        out_specs=(P(CTX, None), P(CTX, exp, None), P(CTX, None)),
        check_vma=False,
    )
```

```python
import functools

import jax
import jax.numpy as jnp
from jax import lax
from jax.experimental import pallas as pl
from jax.experimental.pallas import tpu as pltpu
from jax.sharding import Mesh, PartitionSpec as P

LAT = 512
ROPE = 64
VHEAD = 128
PACK = 4
SLOTS = 8
TOP = 8
EPSILON = 1e-06
SCALE = (VHEAD + ROPE) ** (-0.5)
BF = jnp.bfloat16
F32 = jnp.float32
CTX = ("y", "x", "zl")
EXP = ("zh", "co")
MIB = 1 << 20


def dot(left, right):
    return jnp.dot(left, right, preferred_element_type=F32)


def contract_last(left, right):
    return lax.dot_general(left, right, (((1,), (1,)), ((), ())), preferred_element_type=F32)


def contract_first(left, right):
    return lax.dot_general(left, right, (((0,), (0,)), ((), ())), preferred_element_type=F32)


def call(body, outs, args, vmem_mib, flops=0, scratch=(), far=(), far_out=()):
    size = sum(a.size * a.dtype.itemsize for a in args) + sum(
        o.size * jnp.dtype(o.dtype).itemsize for o in outs
    )

    def place(away):
        return pl.BlockSpec(memory_space=pltpu.HBM if away else pltpu.VMEM)

    return pl.pallas_call(
        body,
        out_shape=tuple(outs),
        in_specs=[pl.BlockSpec(memory_space=pltpu.SMEM)]
        + [place(i in far) for i in range(1, len(args))],
        out_specs=tuple(place(i in far_out) for i in range(len(outs))),
        scratch_shapes=list(scratch),
        compiler_params=pltpu.CompilerParams(vmem_limit_bytes=vmem_mib * MIB),
        cost_estimate=pl.CostEstimate(flops=flops, bytes_accessed=size, transcendentals=0),
    )(*args)


def shape(dims, dtype):
    return jax.ShapeDtypeStruct(dims, dtype)


def prep_kernel(exp_count, pos, *refs):
    far, (send, weight), held, arrived = refs[:6], refs[6:8], refs[8:14], refs[14]
    copies = [
        pltpu.make_async_copy(source, target, arrived.at[i])
        for i, (source, target) in enumerate(zip(far, held))
    ]
    for copy in copies:
        copy.start()
    ids, gates, stream, gain, out_grad, keys = held
    copies[0].wait()
    copies[1].wait()
    rows, width = stream.shape
    slots = weight.shape[0]
    place = lax.broadcasted_iota(jnp.int32, (slots, rows), 0)
    expert = (place // SLOTS) * exp_count + pos[0]
    member = jnp.zeros((slots, rows), F32)
    weighting = jnp.zeros((slots, rows), F32)
    for k in range(ids.shape[0]):
        hit = ids[k : k + 1, :] == expert
        member = jnp.where(hit, 1.0, member)
        weighting = jnp.where(hit, gates[k : k + 1, :], weighting)
    before = (
        lax.broadcasted_iota(jnp.int32, (rows, rows), 0)
        < lax.broadcasted_iota(jnp.int32, (rows, rows), 1)
    ).astype(F32).astype(BF)
    rank = dot(member.astype(BF), before)
    chosen = (member > 0.5) & (rank == (place % SLOTS).astype(F32))
    select = jnp.where(chosen, 1.0, 0.0).astype(BF)
    weight[...] = jnp.where(chosen, weighting, 0.0)
    step = width // 3
    copies[4].wait()
    for c in range(0, width, step):
        send[:, width + c : width + c + step] = dot(select, out_grad[:, c : c + step]).astype(BF)
    copies[2].wait()
    copies[3].wait()
    stream_f = stream[...].astype(F32)
    inv_rms = lax.rsqrt(jnp.mean(stream_f * stream_f, axis=1, keepdims=True) + EPSILON)
    normed = (stream_f * inv_rms * gain[...].astype(F32)).astype(BF)
    for c in range(0, width, step):
        send[:, c : c + step] = dot(select, normed[:, c : c + step]).astype(BF)
    copies[5].wait()
    count = keys.shape[0]
    row = lax.broadcasted_iota(jnp.int32, (slots, count), 0) % SLOTS
    key = lax.broadcasted_iota(jnp.int32, (slots, count), 1)
    ropes = []
    for q in range(PACK):
        wanted = pos[1] * (count // 2) + q * SLOTS + row
        pick = jnp.where(key == wanted, 1.0, 0.0).astype(BF)
        at = 2 * width + q * LAT
        send[:, at : at + LAT] = dot(pick, keys[:, :LAT]).astype(BF)
        ropes.append(dot(pick, keys[:, LAT:]))
    send[:, 2 * width + PACK * LAT :] = jnp.concatenate(ropes, axis=1).astype(BF)


def expert_kernel(pos, rows, w_gate, w_up, w_down_far, grads, key_pack, w_down, arrived):
    width = w_gate.shape[0]
    load = pltpu.make_async_copy(w_down_far, w_down, arrived.at[0])
    load.start()
    store = pltpu.make_async_copy(rows.at[:, 2 * width :], key_pack, arrived.at[1])
    store.start()
    act_gate = dot(rows[:, :width], w_gate[...])
    act_up = dot(rows[:, :width], w_up[...])
    load.wait()
    hidden_back = contract_last(rows[:, width : 2 * width], w_down[...])
    sig = jax.nn.sigmoid(act_gate)
    gate_back = (hidden_back * act_up * sig * (1.0 + act_gate * (1.0 - sig))).astype(BF)
    up_back = (hidden_back * act_gate * sig).astype(BF)
    step = width // 3
    for c in range(0, width, step):
        grads[:, c : c + step] = (
            contract_last(gate_back, w_gate[c : c + step, :])
            + contract_last(up_back, w_up[c : c + step, :])
        ).astype(BF)
    store.wait()


def combine_kernel(pos, returned, weight, keep, send, total):
    half = keep.shape[0]
    w = weight[...]
    high = w.astype(BF)
    low = (w - high.astype(F32)).astype(BF)
    both = jnp.concatenate([high, low], axis=0)
    width = returned.shape[1]
    step = width // 3
    for c in range(0, width, step):
        part = returned[:, c : c + step]
        total[:, c : c + step] = contract_first(both, jnp.concatenate([part, part], axis=0))
    piece = half // 4

    def rows(chip, side, count):
        return pl.ds(pl.multiple_of((chip * 2 + side) * piece, piece), count)

    core, chip = pos[1], pos[2]
    across = lax.rem(chip + 2, 4)
    for side, out in ((core, keep), (1 - core, send)):
        beside = lax.rem(chip + 1 + 2 * side, 4)
        out[:piece, :] = total[rows(chip, side, piece), :].astype(out.dtype)
        out[piece : 2 * piece, :] = total[rows(across, side, piece), :].astype(out.dtype)
        out[2 * piece :, :] = total[rows(beside, 0, 2 * piece), :].astype(out.dtype)


def pair_kernel(pos, keep, received, own, across, beside):
    total = (keep[...] + received[...].astype(F32)).astype(BF)
    piece = own.shape[0]
    own[...] = total[:piece, :]
    across[...] = total[piece : 2 * piece, :]
    beside[...] = total[2 * piece :, :]


def stream_kernel(
    pos, own, own_2, beside, beside_2, across, across_2, stream, gain, out_grad, stream_grad, half_grad
):
    first = pos[1] == 0
    piece, width = own.shape
    rows = 2 * piece

    def ordered(mine, other):
        a, b = mine[...].astype(F32), other[...].astype(F32)
        return jnp.where(first, a, b), jnp.where(first, b, a)

    below, above = ordered(beside, beside_2)
    normed_grad = jnp.concatenate(ordered(own, own_2), axis=0) + below + above
    normed_grad = normed_grad + jnp.concatenate(ordered(across, across_2), axis=0)
    here = pl.ds(pl.multiple_of(pos[2] * rows, rows), rows)
    stream_f = stream[here, :].astype(F32)
    gain_f = gain[...].astype(F32)
    inv_rms = lax.rsqrt(jnp.mean(stream_f * stream_f, axis=1, keepdims=True) + EPSILON)
    scaled = normed_grad * gain_f
    branch = inv_rms * scaled - stream_f * (inv_rms * inv_rms * inv_rms) * jnp.mean(
        scaled * stream_f, axis=1, keepdims=True
    )
    result = (out_grad[here, :].astype(F32) + branch).astype(BF)
    stream_grad[...] = result
    half_grad[...] = jnp.where(first, result[:piece, :], result[piece:, :])


def latent_kernel(
    pos,
    own,
    beside,
    beside_2,
    across,
    across_2,
    out_proj,
    value_up,
    latent_out,
    stream_far,
    latent_t,
    latent_rows,
    delta,
    stream_grad,
    sent,
):
    core, chip = pos[1], pos[2]
    piece = across.shape[0]

    def put(value, place, side):
        at = pl.multiple_of((lax.rem(chip + place, 4) * 2 + side) * piece, piece)
        stream_grad[pl.ds(at, value.shape[0]), :] = value[...]

    put(own, 0, 0)
    put(beside, 3 + 2 * core, 0)
    put(beside_2, 1 + 2 * core, 0)
    put(across, 2, core)
    put(across_2, 2, 1 - core)
    store = pltpu.make_async_copy(stream_grad, stream_far, sent.at[0])
    store.start()
    heads, lat, vhead = value_up.shape
    count = stream_grad.shape[0]
    all_rows = stream_grad[...]
    for h in range(heads):
        head_t = contract_last(out_proj[h], all_rows).astype(BF)
        grad_t = dot(value_up[h], head_t).astype(BF)
        cols = slice(h * count, (h + 1) * count)
        latent_t[:, cols] = grad_t
        grad_f = grad_t.astype(F32)
        delta[:, cols] = jnp.sum(grad_f * latent_out[:, cols], axis=0, keepdims=True)
        latent_rows[cols, :] = grad_f.T.astype(BF)
    store.wait()


def rope_lanes(q):
    at = PACK * LAT + (q // 2) * 2 * ROPE
    return slice(at, at + 2 * ROPE)


def scores_kernel(
    pos,
    mine_far,
    other_far,
    queries_t,
    seen,
    probs_far,
    latent_far,
    rows_far,
    mine,
    other,
    scratch,
    probs,
    latent_out,
    query_rows,
    arrived,
):
    heads, width, rows = queries_t.shape
    slots = mine.shape[0]
    count = heads * rows
    loads = [
        pltpu.make_async_copy(mine_far, mine, arrived.at[0]),
        pltpu.make_async_copy(other_far, other, arrived.at[1]),
    ]
    for load in loads:
        load.start()
    blank = jnp.zeros((ROPE, count), BF)
    query = jnp.concatenate([queries_t[h] for h in range(heads)], axis=1)
    rope = query[LAT:, :]
    ropes = [jnp.concatenate([rope, blank], axis=0), jnp.concatenate([blank, rope], axis=0)]
    stacked = jnp.concatenate([query[:LAT, :]] + ropes, axis=0)
    query_rows[...] = stacked.astype(F32).T.astype(BF)
    stores = [pltpu.make_async_copy(query_rows, rows_far, arrived.at[2])]
    stores[0].start()
    last = jnp.concatenate([seen[...]] * heads, axis=1)
    place = lax.broadcasted_iota(jnp.int32, (slots, 1), 0)
    slot_key = (place // SLOTS) * (2 * PACK * SLOTS) + place % SLOTS
    top = jnp.full((1, count), -jnp.inf, F32)
    for side, keys in enumerate((mine, other)):
        loads[side].wait()
        core = pos[1] if side == 0 else 1 - pos[1]
        for q in range(PACK):
            s = dot(keys[:, q * LAT : (q + 1) * LAT], query[:LAT, :])
            s = (s + dot(keys[:, rope_lanes(q)], ropes[q % 2])) * SCALE
            key = slot_key + (core * (PACK * SLOTS) + q * SLOTS)
            s = jnp.where(key <= last, s, -jnp.inf)
            scratch[side * PACK + q] = s
            top = jnp.maximum(top, jnp.max(s, axis=0, keepdims=True))
    total = jnp.zeros((1, count), F32)
    for c in range(2 * PACK):
        e = jnp.exp(scratch[c] - top)
        scratch[c] = e
        total = total + jnp.sum(e, axis=0, keepdims=True)
    inverse = 1.0 / total
    for c in range(2 * PACK):
        q = c % PACK
        p = (scratch[c] * inverse).astype(BF)
        probs[c] = p
        store = pltpu.make_async_copy(probs.at[c], probs_far.at[c], arrived.at[3 + c])
        store.start()
        stores.append(store)
        part = contract_first((mine if c < PACK else other)[:, q * LAT : (q + 1) * LAT], p)
        if c == 0:
            latent_out[...] = part
        else:
            latent_out[...] += part
    store = pltpu.make_async_copy(latent_out, latent_far, arrived.at[3 + 2 * PACK])
    store.start()
    for store in stores + [store]:
        store.wait()


def score_gradient(keys, p, q, latent_t, delta):
    prob_grad = dot(keys[:, q * LAT : (q + 1) * LAT], latent_t)
    return (p.astype(F32) * (prob_grad - delta) * SCALE).astype(BF)


def back_kernel(side, pos, keys, probs, latent_t, latent_rows, delta, query_rows, key_grad):
    part = []
    for q in range(PACK):
        p = probs[side * PACK + q]
        sg = score_gradient(keys, p, q, latent_t[...], delta[...])
        key_grad[:, q * LAT : (q + 1) * LAT] = (
            dot(sg, query_rows[:, :LAT]) + dot(p, latent_rows[...])
        ).astype(BF)
        at = LAT + (q % 2) * 2 * ROPE
        part.append(dot(sg, query_rows[:, at : at + 2 * ROPE]))
        if q % 2:
            key_grad[:, rope_lanes(q)] = (part[q - 1] + part[q]).astype(BF)


def query_kernel(pos, mine, other, probs, latent_t, delta, out):
    heads, width, rows = out.shape
    for pair in range(heads // 2):
        cols = slice(2 * pair * rows, 2 * (pair + 1) * rows)
        total = rope = None
        for side, keys in enumerate((mine, other)):
            for q in range(PACK):
                p = probs[side * PACK + q, :, cols]
                sg = score_gradient(keys, p, q, latent_t[:, cols], delta[:, cols])
                lat_part = contract_first(keys[:, q * LAT : (q + 1) * LAT], sg)
                rope_part = contract_first(keys[:, rope_lanes(q)], sg)
                rope_part = rope_part[(q % 2) * ROPE : (q % 2 + 1) * ROPE, :]
                total = lat_part if total is None else total + lat_part
                rope = rope_part if rope is None else rope + rope_part
        for i in range(2):
            own = slice(i * rows, (i + 1) * rows)
            out[2 * pair + i] = jnp.concatenate([total[:, own], rope[:, own]], axis=0).astype(BF)


def add_kernel(pos, left, right, out):
    out[...] = (left[...].astype(F32) + right[...].astype(F32)).astype(BF)


def sum_kernel(pos, parts, out):
    count, width = parts.shape
    spread = parts[...].astype(F32).reshape(count // SLOTS, SLOTS, width)
    out[...] = jnp.sum(spread, axis=0).astype(BF)


def final_kernel(pos, parts, out):
    spread = parts[...].astype(F32)
    rows = []
    for core in range(2):
        total = None
        for z in range(4):
            at = (2 * z + core) * SLOTS
            part = spread[at : at + SLOTS, :]
            total = part if total is None else total + part
        for q in range(PACK):
            at = PACK * LAT + q * ROPE
            rows.append(
                jnp.concatenate([total[:, q * LAT : (q + 1) * LAT], total[:, at : at + ROPE]], axis=1)
            )
    out[...] = jnp.concatenate(rows, axis=0).astype(BF)


def swap(value):
    return lax.ppermute(value, "co", [(0, 1), (1, 0)])


def turn_beside(value):
    steps = [(2 * z + c, 2 * ((z + 1 + 2 * c) % 4) + c) for z in range(4) for c in range(2)]
    return lax.ppermute(value, EXP, steps)


def turn_across(value):
    return lax.ppermute(value, "zh", [(z, (z + 2) % 4) for z in range(4)])


def exchange(value):
    return lax.all_to_all(value, CTX, split_axis=0, concat_axis=0, tiled=True)


def shards(
    queries,
    key_latents,
    query_pos,
    value_up,
    out_proj,
    stream,
    norm_gain,
    expert_ids,
    gate_weights,
    w_gate,
    w_up,
    w_down,
    out_grad,
):
    ctx_count = lax.axis_size(CTX)
    exp_count = lax.axis_size("zh") * lax.axis_size("co")
    rows, width = stream.shape
    slots = ctx_count * SLOTS
    core = lax.axis_index("co")
    group = lax.axis_index("zh")
    pos = jnp.stack([group * 2 + core, core, group]).astype(jnp.int32)
    gain = norm_gain.reshape(1, width)
    hidden = w_gate.shape[2]

    key_count, key_width = key_latents.shape
    send, weight = call(
        functools.partial(prep_kernel, exp_count),
        [shape((slots, 3 * width), BF), shape((slots, rows), F32)],
        [pos, expert_ids.T, gate_weights.T, stream, gain, out_grad, key_latents],
        58,
        flops=4 * slots * rows * width,
        scratch=[
            pltpu.VMEM((TOP, rows), jnp.int32),
            pltpu.VMEM((TOP, rows), F32),
            pltpu.VMEM((rows, width), BF),
            pltpu.VMEM((1, width), BF),
            pltpu.VMEM((rows, width), BF),
            pltpu.VMEM((key_count, key_width), BF),
            pltpu.SemaphoreType.DMA((6,)),
        ],
        far=range(1, 7),
    )
    arrived = exchange(send.reshape(ctx_count, SLOTS, 3 * width)).reshape(slots, 3 * width)
    grads, mine = call(
        expert_kernel,
        [shape((slots, width), BF), shape((slots, width), BF)],
        [pos, arrived, w_gate[0], w_up[0], w_down[0]],
        12,
        flops=10 * slots * width * hidden,
        scratch=[pltpu.VMEM((hidden, width), BF), pltpu.SemaphoreType.DMA((2,))],
        far=(4,),
        far_out=(1,),
    )
    returned = exchange(grads.reshape(ctx_count, SLOTS, width))
    other = swap(mine)
    heads = queries.shape[1]
    flat = heads * rows
    half = slots * PACK
    wide = LAT + 4 * ROPE
    probs, latent_out, query_rows = call(
        scores_kernel,
        [
            shape((2 * PACK, slots, flat), BF),
            shape((LAT, flat), F32),
            shape((flat, wide), BF),
        ],
        [pos, mine, other, jnp.transpose(queries, (1, 2, 0)), query_pos.reshape(1, rows)],
        24,
        flops=4 * half * flat * (key_width + LAT),
        scratch=[
            pltpu.VMEM((slots, width), BF),
            pltpu.VMEM((slots, width), BF),
            pltpu.VMEM((2 * PACK, slots, flat), F32),
            pltpu.VMEM((2 * PACK, slots, flat), BF),
            pltpu.VMEM((LAT, flat), F32),
            pltpu.VMEM((flat, wide), BF),
            pltpu.SemaphoreType.DMA((4 + 2 * PACK,)),
        ],
        far=(1, 2),
        far_out=(0, 1, 2),
    )
    returned, probs, latent_out, query_rows = lax.optimization_barrier(
        (returned, probs, latent_out, query_rows)
    )
    returned = returned.reshape(slots, width)

    keep, other_part = call(
        combine_kernel,
        [shape((rows // 2, width), F32), shape((rows // 2, width), BF)],
        [pos, returned, weight],
        8,
        flops=8 * slots * rows * width,
        scratch=[pltpu.VMEM((rows, width), F32)],
    )
    received = swap(other_part)
    piece = rows // 8
    own, across, beside = call(
        pair_kernel,
        [shape((piece, width), BF), shape((piece, width), BF), shape((2 * piece, width), BF)],
        [pos, keep, received],
        4,
    )
    beside, across = turn_beside(beside), turn_across(across)
    own_grad, half_grad = call(
        stream_kernel,
        [shape((2 * piece, width), BF), shape((piece, width), BF)],
        [pos, own, swap(own), beside, swap(beside), across, swap(across), stream, gain, out_grad],
        4,
    )
    beside, across = turn_beside(own_grad), turn_across(half_grad)
    stream_grad, latent_t, latent_rows, delta = call(
        latent_kernel,
        [
            shape((rows, width), BF),
            shape((LAT, flat), BF),
            shape((flat, LAT), BF),
            shape((1, flat), F32),
        ],
        [
            pos,
            own_grad,
            beside,
            swap(beside),
            across,
            swap(across),
            out_proj,
            value_up,
            latent_out,
        ],
        8,
        flops=2 * flat * VHEAD * (width + LAT),
        scratch=[pltpu.VMEM((rows, width), BF), pltpu.SemaphoreType.DMA((1,))],
        far_out=(0,),
    )

    def back(side, keys):
        (key_part,) = call(
            functools.partial(back_kernel, side),
            [shape((slots, width), BF)],
            [pos, keys, probs, latent_t, latent_rows, delta, query_rows],
            8,
            flops=2 * half * flat * (2 * LAT + key_width),
        )
        return key_part

    key_received = swap(back(1, other))
    key_mine = back(0, mine)
    (key_sum,) = call(add_kernel, [shape((slots, width), BF)], [pos, key_mine, key_received], 4)
    key_parts = exchange(key_sum.reshape(ctx_count, SLOTS, width))
    (query_grad_t,) = call(
        query_kernel,
        [shape((heads, key_width, rows), BF)],
        [pos, mine, other, probs, latent_t, delta],
        16,
        flops=4 * half * flat * (key_width + LAT),
    )
    key_parts, query_grad_t = lax.optimization_barrier((key_parts, query_grad_t))
    query_grad = jnp.transpose(query_grad_t, (2, 0, 1))
    (key_own,) = call(
        sum_kernel, [shape((SLOTS, width), BF)], [pos, key_parts.reshape(slots, width)], 8
    )
    (key_grad,) = call(
        final_kernel,
        [shape((key_count, key_width), BF)],
        [pos, lax.all_gather(key_own, EXP, axis=0, tiled=True)],
        4,
    )
    return (stream_grad, query_grad, key_grad)


def solution(mesh):
    fine = Mesh(mesh.devices.reshape(4, 4, 2, 4, 2), ("y", "x", "zl", "zh", "co"))
    exp = EXP
    both = CTX + exp
    placed = (
        P(CTX, exp, None),
        P(CTX, None),
        P(CTX),
        P(exp, None, None),
        P(exp, None, None),
        P(CTX, None),
        P(),
        P(CTX, None),
        P(CTX, None),
        P(both, None, None),
        P(both, None, None),
        P(both, None, None),
        P(CTX, None),
    )
    return jax.shard_map(
        shards,
        mesh=fine,
        in_specs=placed,
        out_specs=(P(CTX, None), P(CTX, exp, None), P(CTX, None)),
        check_vma=False,
    )
```

```python
import functools

import jax
import jax.numpy as jnp
from jax import lax
from jax.experimental import pallas as pl
from jax.experimental.pallas import tpu as pltpu
from jax.sharding import Mesh, PartitionSpec as P

LAT = 512
ROPE = 64
VHEAD = 128
PACK = 4
SLOTS = 8
TOP = 8
EPSILON = 1e-06
SCALE = (VHEAD + ROPE) ** (-0.5)
BF = jnp.bfloat16
F32 = jnp.float32
CTX = ("y", "x", "zl")
EXP = ("zh", "co")
MIB = 1 << 20


def dot(left, right):
    return jnp.dot(left, right, preferred_element_type=F32)


def contract_last(left, right):
    return lax.dot_general(left, right, (((1,), (1,)), ((), ())), preferred_element_type=F32)


def contract_first(left, right):
    return lax.dot_general(left, right, (((0,), (0,)), ((), ())), preferred_element_type=F32)


def call(body, outs, args, vmem_mib, flops=0, scratch=(), far=(), far_out=()):
    size = sum(a.size * a.dtype.itemsize for a in args) + sum(
        o.size * jnp.dtype(o.dtype).itemsize for o in outs
    )

    def place(away):
        return pl.BlockSpec(memory_space=pltpu.HBM if away else pltpu.VMEM)

    return pl.pallas_call(
        body,
        out_shape=tuple(outs),
        in_specs=[place(i in far) for i in range(len(args))],
        out_specs=tuple(place(i in far_out) for i in range(len(outs))),
        scratch_shapes=list(scratch),
        compiler_params=pltpu.CompilerParams(vmem_limit_bytes=vmem_mib * MIB),
        cost_estimate=pl.CostEstimate(flops=flops, bytes_accessed=size, transcendentals=0),
    )(*args)


def shape(dims, dtype):
    return jax.ShapeDtypeStruct(dims, dtype)


def position():
    core, group = lax.axis_index("co"), lax.axis_index("zh")
    return group * 2 + core, core, group


def spread(row_ref):
    rows = row_ref[...].astype(F32)
    return jnp.concatenate([rows[i : i + 1, :] for i in range(rows.shape[0])], axis=1)


def prep_kernel(exp_count, *refs):
    pos = position()
    far, (send, weight), held, arrived = refs[:6], refs[6:8], refs[8:14], refs[14]
    copies = [
        pltpu.make_async_copy(source, target, arrived.at[i])
        for i, (source, target) in enumerate(zip(far, held))
    ]
    for copy in copies:
        copy.start()
    ids, gates, stream, gain, out_grad, keys = held
    copies[0].wait()
    copies[1].wait()
    rows, width = stream.shape
    slots = weight.shape[0]
    place = lax.broadcasted_iota(jnp.int32, (slots, rows), 0)
    expert = (place // SLOTS) * exp_count + pos[0]
    member = jnp.zeros((slots, rows), F32)
    weighting = jnp.zeros((slots, rows), F32)
    for k in range(ids.shape[0]):
        hit = ids[k : k + 1, :] == expert
        member = jnp.where(hit, 1.0, member)
        weighting = jnp.where(hit, gates[k : k + 1, :], weighting)
    before = (
        lax.broadcasted_iota(jnp.int32, (rows, rows), 0)
        < lax.broadcasted_iota(jnp.int32, (rows, rows), 1)
    ).astype(F32).astype(BF)
    rank = dot(member.astype(BF), before)
    chosen = (member > 0.5) & (rank == (place % SLOTS).astype(F32))
    select = jnp.where(chosen, 1.0, 0.0).astype(BF)
    weight[...] = jnp.where(chosen, weighting, 0.0)
    step = width // 3
    copies[4].wait()
    for c in range(0, width, step):
        send[:, width + c : width + c + step] = dot(select, out_grad[:, c : c + step]).astype(BF)
    copies[2].wait()
    copies[3].wait()
    stream_f = stream[...].astype(F32)
    inv_rms = lax.rsqrt(jnp.mean(stream_f * stream_f, axis=1, keepdims=True) + EPSILON)
    normed = (stream_f * inv_rms * spread(gain)).astype(BF)
    for c in range(0, width, step):
        send[:, c : c + step] = dot(select, normed[:, c : c + step]).astype(BF)
    copies[5].wait()
    count = keys.shape[0]
    row = lax.broadcasted_iota(jnp.int32, (SLOTS, count), 0)
    key = lax.broadcasted_iota(jnp.int32, (SLOTS, count), 1)
    parts, ropes = [], []
    for q in range(PACK):
        wanted = pos[1] * (count // 2) + q * SLOTS + row
        pick = jnp.where(key == wanted, 1.0, 0.0).astype(BF)
        parts.append(dot(pick, keys[:, :LAT]))
        ropes.append(dot(pick, keys[:, LAT:]))
    parts.append(jnp.concatenate(ropes, axis=1))
    at = 2 * width
    for part in parts:
        wide = part.shape[1]
        part = jnp.broadcast_to(part[None], (slots // SLOTS, SLOTS, wide))
        send[:, at : at + wide] = part.reshape(slots, wide).astype(BF)
        at += wide


def expert_kernel(rows, w_gate, w_up, w_down_far, grads, key_pack, w_down, arrived):
    width = w_gate.shape[0]
    load = pltpu.make_async_copy(w_down_far, w_down, arrived.at[0])
    load.start()
    store = pltpu.make_async_copy(rows.at[:, 2 * width :], key_pack, arrived.at[1])
    store.start()
    act_gate = dot(rows[:, :width], w_gate[...])
    act_up = dot(rows[:, :width], w_up[...])
    load.wait()
    hidden_back = contract_last(rows[:, width : 2 * width], w_down[...])
    sig = jax.nn.sigmoid(act_gate)
    gate_back = (hidden_back * act_up * sig * (1.0 + act_gate * (1.0 - sig))).astype(BF)
    up_back = (hidden_back * act_gate * sig).astype(BF)
    step = width // 3
    for c in range(0, width, step):
        grads[:, c : c + step] = (
            contract_last(gate_back, w_gate[c : c + step, :])
            + contract_last(up_back, w_up[c : c + step, :])
        ).astype(BF)
    store.wait()


def order_kernel(weight, ordered):
    pos = position()
    w = weight[...]
    high = w.astype(BF)
    low = (w - high.astype(F32)).astype(BF)
    rows = w.shape[1]
    piece = rows // 8
    core, chip = pos[1], pos[2]
    place = lax.broadcasted_iota(jnp.int32, (1, rows), 1)
    part, within = (place // piece) % 4, place % piece
    side = jnp.where(place < rows // 2, core, 1 - core)
    at_chip = jnp.where(part == 0, chip, jnp.where(part == 1, chip + 2, chip + 1 + 2 * side)) % 4
    half = jnp.where(part < 2, side, part - 2)
    source = (at_chip * 2 + half) * piece + within
    index = lax.broadcasted_iota(jnp.int32, (rows, rows), 0)
    moved = jnp.where(index == source, 1.0, 0.0).astype(BF)
    slots = w.shape[0]
    ordered[:slots, :] = dot(high, moved).astype(BF)
    ordered[slots:, :] = dot(low, moved).astype(BF)


def combine_kernel(returned, ordered, keep, send):
    half, width = keep.shape
    weights = ordered[...]
    step = width // 3
    for c in range(0, width, step):
        part = returned[:, c : c + step]
        total = contract_first(weights, jnp.concatenate([part, part], axis=0))
        keep[:, c : c + step] = total[:half, :]
        send[:, c : c + step] = total[half:, :].astype(BF)


def pair_kernel(keep, received, own, across, beside):
    total = (keep[...] + received[...].astype(F32)).astype(BF)
    piece = own.shape[0]
    own[...] = total[:piece, :]
    across[...] = total[piece : 2 * piece, :]
    beside[...] = total[2 * piece :, :]


def stream_kernel(
    own, own_2, beside, beside_2, across, across_2, stream, gain, out_grad, stream_grad, half_grad
):
    pos = position()
    first = pos[1] == 0
    piece, width = own.shape
    rows = 2 * piece

    def ordered(mine, other):
        a, b = mine[...].astype(F32), other[...].astype(F32)
        return jnp.where(first, a, b), jnp.where(first, b, a)

    below, above = ordered(beside, beside_2)
    normed_grad = jnp.concatenate(ordered(own, own_2), axis=0) + below + above
    normed_grad = normed_grad + jnp.concatenate(ordered(across, across_2), axis=0)
    here = pl.ds(pl.multiple_of(pos[2] * rows, rows), rows)
    stream_f = stream[here, :].astype(F32)
    gain_f = spread(gain)
    inv_rms = lax.rsqrt(jnp.mean(stream_f * stream_f, axis=1, keepdims=True) + EPSILON)
    scaled = normed_grad * gain_f
    branch = inv_rms * scaled - stream_f * (inv_rms * inv_rms * inv_rms) * jnp.mean(
        scaled * stream_f, axis=1, keepdims=True
    )
    result = (out_grad[here, :].astype(F32) + branch).astype(BF)
    stream_grad[...] = result
    half_grad[...] = jnp.where(first, result[:piece, :], result[piece:, :])


def latent_kernel(
    own,
    beside,
    beside_2,
    across,
    across_2,
    out_proj,
    value_up,
    latent_out,
    stream_far,
    latent_t,
    latent_rows,
    delta,
    stream_grad,
    sent,
):
    _, core, chip = position()
    piece = across.shape[0]

    def put(value, place, side):
        at = pl.multiple_of((lax.rem(chip + place, 4) * 2 + side) * piece, piece)
        stream_grad[pl.ds(at, value.shape[0]), :] = value[...]

    put(own, 0, 0)
    put(beside, 3 + 2 * core, 0)
    put(beside_2, 1 + 2 * core, 0)
    put(across, 2, core)
    put(across_2, 2, 1 - core)
    store = pltpu.make_async_copy(stream_grad, stream_far, sent.at[0])
    store.start()
    heads, lat, vhead = value_up.shape
    count = stream_grad.shape[0]
    all_rows = stream_grad[...]
    for h in range(heads):
        head_t = contract_last(out_proj[h], all_rows).astype(BF)
        grad_t = dot(value_up[h], head_t).astype(BF)
        cols = slice(h * count, (h + 1) * count)
        latent_t[:, cols] = grad_t
        grad_f = grad_t.astype(F32)
        delta[:, cols] = jnp.sum(grad_f * latent_out[:, cols], axis=0, keepdims=True)
        latent_rows[cols, :] = grad_f.T.astype(BF)
    store.wait()


def rope_lanes(q):
    at = PACK * LAT + (q // 2) * 2 * ROPE
    return slice(at, at + 2 * ROPE)


def scores_kernel(
    mine_far,
    other_far,
    queries_t,
    seen,
    probs_far,
    latent_far,
    rows_far,
    mine,
    other,
    scratch,
    probs,
    latent_out,
    query_rows,
    arrived,
):
    pos = position()
    heads, width, rows = queries_t.shape
    slots = mine.shape[0]
    count = heads * rows
    loads = [
        pltpu.make_async_copy(mine_far, mine, arrived.at[0]),
        pltpu.make_async_copy(other_far, other, arrived.at[1]),
    ]
    for load in loads:
        load.start()
    blank = jnp.zeros((ROPE, count), BF)
    query = jnp.concatenate([queries_t[h] for h in range(heads)], axis=1)
    rope = query[LAT:, :]
    ropes = [jnp.concatenate([rope, blank], axis=0), jnp.concatenate([blank, rope], axis=0)]
    stacked = jnp.concatenate([query[:LAT, :]] + ropes, axis=0)
    query_rows[...] = stacked.astype(F32).T.astype(BF)
    stores = [pltpu.make_async_copy(query_rows, rows_far, arrived.at[2])]
    stores[0].start()
    last = jnp.concatenate([seen[...]] * heads, axis=1)
    place = lax.broadcasted_iota(jnp.int32, (slots, 1), 0)
    slot_key = (place // SLOTS) * (2 * PACK * SLOTS) + place % SLOTS
    top = jnp.full((1, count), -jnp.inf, F32)
    for side, keys in enumerate((mine, other)):
        loads[side].wait()
        core = pos[1] if side == 0 else 1 - pos[1]
        for q in range(PACK):
            s = dot(keys[:, q * LAT : (q + 1) * LAT], query[:LAT, :])
            s = (s + dot(keys[:, rope_lanes(q)], ropes[q % 2])) * SCALE
            key = slot_key + (core * (PACK * SLOTS) + q * SLOTS)
            s = jnp.where(key <= last, s, -jnp.inf)
            scratch[side * PACK + q] = s
            top = jnp.maximum(top, jnp.max(s, axis=0, keepdims=True))
    total = jnp.zeros((1, count), F32)
    for c in range(2 * PACK):
        e = jnp.exp(scratch[c] - top)
        scratch[c] = e
        total = total + jnp.sum(e, axis=0, keepdims=True)
    inverse = 1.0 / total
    for c in range(2 * PACK):
        q = c % PACK
        p = (scratch[c] * inverse).astype(BF)
        probs[c] = p
        store = pltpu.make_async_copy(probs.at[c], probs_far.at[c], arrived.at[3 + c])
        store.start()
        stores.append(store)
        part = contract_first((mine if c < PACK else other)[:, q * LAT : (q + 1) * LAT], p)
        if c == 0:
            latent_out[...] = part
        else:
            latent_out[...] += part
    store = pltpu.make_async_copy(latent_out, latent_far, arrived.at[3 + 2 * PACK])
    store.start()
    for store in stores + [store]:
        store.wait()


def score_gradient(keys, p, q, latent_t, delta):
    prob_grad = dot(keys[:, q * LAT : (q + 1) * LAT], latent_t)
    return (p.astype(F32) * (prob_grad - delta) * SCALE).astype(BF)


def back_kernel(side, keys, probs, latent_t, latent_rows, delta, query_rows, key_grad):
    part = []
    for q in range(PACK):
        p = probs[side * PACK + q]
        sg = score_gradient(keys, p, q, latent_t[...], delta[...])
        key_grad[:, q * LAT : (q + 1) * LAT] = (
            dot(sg, query_rows[:, :LAT]) + dot(p, latent_rows[...])
        ).astype(BF)
        at = LAT + (q % 2) * 2 * ROPE
        part.append(dot(sg, query_rows[:, at : at + 2 * ROPE]))
        if q % 2:
            key_grad[:, rope_lanes(q)] = (part[q - 1] + part[q]).astype(BF)


def query_kernel(mine, other, probs, latent_t, delta, out):
    heads, width, rows = out.shape
    for pair in range(heads // 2):
        cols = slice(2 * pair * rows, 2 * (pair + 1) * rows)
        total = rope = None
        for side, keys in enumerate((mine, other)):
            for q in range(PACK):
                p = probs[side * PACK + q, :, cols]
                sg = score_gradient(keys, p, q, latent_t[:, cols], delta[:, cols])
                lat_part = contract_first(keys[:, q * LAT : (q + 1) * LAT], sg)
                rope_part = contract_first(keys[:, rope_lanes(q)], sg)
                rope_part = rope_part[(q % 2) * ROPE : (q % 2 + 1) * ROPE, :]
                total = lat_part if total is None else total + lat_part
                rope = rope_part if rope is None else rope + rope_part
        for i in range(2):
            own = slice(i * rows, (i + 1) * rows)
            out[2 * pair + i] = jnp.concatenate([total[:, own], rope[:, own]], axis=0).astype(BF)


def add_kernel(left, right, out):
    out[...] = (left[...].astype(F32) + right[...].astype(F32)).astype(BF)


def sum_kernel(parts, out):
    count, width = parts.shape
    spread = parts[...].astype(F32).reshape(count // SLOTS, SLOTS, width)
    out[...] = jnp.sum(spread, axis=0).astype(BF)


def join_kernel(own, near, out):
    pos = position()
    first = pos[1] == 0
    a, b = own[...].astype(F32), near[...].astype(F32)
    out[...] = jnp.concatenate([jnp.where(first, a, b), jnp.where(first, b, a)], axis=0).astype(BF)


def final_kernel(own, beside, beside_2, across, across_2, out, chips):
    pos = position()
    first, chip = pos[1] == 0, pos[2]
    a, b = across[...].astype(F32), across_2[...].astype(F32)
    chips[chip] = own[...].astype(F32)
    chips[lax.rem(chip + 3 + 2 * pos[1], 4)] = beside[...].astype(F32)
    chips[lax.rem(chip + 1 + 2 * pos[1], 4)] = beside_2[...].astype(F32)
    chips[lax.rem(chip + 2, 4)] = jnp.concatenate(
        [jnp.where(first, a, b), jnp.where(first, b, a)], axis=0
    )
    total = ((chips[0] + chips[1]) + chips[2]) + chips[3]
    rows = []
    for core in range(2):
        part = total[core * SLOTS : (core + 1) * SLOTS, :]
        for q in range(PACK):
            at = PACK * LAT + q * ROPE
            rows.append(
                jnp.concatenate([part[:, q * LAT : (q + 1) * LAT], part[:, at : at + ROPE]], axis=1)
            )
    out[...] = jnp.concatenate(rows, axis=0).astype(BF)


def swap(value):
    return lax.ppermute(value, "co", [(0, 1), (1, 0)])


def turn_beside(value):
    steps = [(2 * z + c, 2 * ((z + 1 + 2 * c) % 4) + c) for z in range(4) for c in range(2)]
    return lax.ppermute(value, EXP, steps)


def turn_across(value):
    return lax.ppermute(value, "zh", [(z, (z + 2) % 4) for z in range(4)])


def exchange(value):
    return lax.all_to_all(value, CTX, split_axis=0, concat_axis=0, tiled=True)


def shards(
    queries,
    key_latents,
    query_pos,
    value_up,
    out_proj,
    stream,
    norm_gain,
    expert_ids,
    gate_weights,
    w_gate,
    w_up,
    w_down,
    out_grad,
):
    ctx_count = lax.axis_size(CTX)
    exp_count = lax.axis_size("zh") * lax.axis_size("co")
    rows, width = stream.shape
    slots = ctx_count * SLOTS
    gain = norm_gain.reshape(width // 128, 128)
    hidden = w_gate.shape[2]

    key_count, key_width = key_latents.shape
    send, weight = call(
        functools.partial(prep_kernel, exp_count),
        [shape((slots, 3 * width), BF), shape((slots, rows), F32)],
        [expert_ids.T, gate_weights.T, stream, gain, out_grad, key_latents],
        58,
        flops=4 * slots * rows * width,
        scratch=[
            pltpu.VMEM((TOP, rows), jnp.int32),
            pltpu.VMEM((TOP, rows), F32),
            pltpu.VMEM((rows, width), BF),
            pltpu.VMEM(gain.shape, BF),
            pltpu.VMEM((rows, width), BF),
            pltpu.VMEM((key_count, key_width), BF),
            pltpu.SemaphoreType.DMA((6,)),
        ],
        far=range(6),
    )
    arrived = exchange(send.reshape(ctx_count, SLOTS, 3 * width)).reshape(slots, 3 * width)
    grads, mine = call(
        expert_kernel,
        [shape((slots, width), BF), shape((slots, width), BF)],
        [arrived, w_gate[0], w_up[0], w_down[0]],
        12,
        flops=10 * slots * width * hidden,
        scratch=[pltpu.VMEM((hidden, width), BF), pltpu.SemaphoreType.DMA((2,))],
        far=(3,),
        far_out=(1,),
    )
    returned = exchange(grads.reshape(ctx_count, SLOTS, width))
    other = swap(mine)
    heads = queries.shape[1]
    flat = heads * rows
    half = slots * PACK
    wide = LAT + 4 * ROPE
    probs, latent_out, query_rows = call(
        scores_kernel,
        [
            shape((2 * PACK, slots, flat), BF),
            shape((LAT, flat), F32),
            shape((flat, wide), BF),
        ],
        [mine, other, jnp.transpose(queries, (1, 2, 0)), query_pos.reshape(1, rows)],
        24,
        flops=4 * half * flat * (key_width + LAT),
        scratch=[
            pltpu.VMEM((slots, width), BF),
            pltpu.VMEM((slots, width), BF),
            pltpu.VMEM((2 * PACK, slots, flat), F32),
            pltpu.VMEM((2 * PACK, slots, flat), BF),
            pltpu.VMEM((LAT, flat), F32),
            pltpu.VMEM((flat, wide), BF),
            pltpu.SemaphoreType.DMA((4 + 2 * PACK,)),
        ],
        far=(0, 1),
        far_out=(0, 1, 2),
    )
    (ordered,) = call(order_kernel, [shape((2 * slots, rows), BF)], [weight], 4)
    returned, probs, latent_out, query_rows, ordered = lax.optimization_barrier(
        (returned, probs, latent_out, query_rows, ordered)
    )
    returned = returned.reshape(slots, width)

    keep, other_part = call(
        combine_kernel,
        [shape((rows // 2, width), F32), shape((rows // 2, width), BF)],
        [returned, ordered],
        8,
        flops=8 * slots * rows * width,
    )
    received = swap(other_part)
    piece = rows // 8
    own, across, beside = call(
        pair_kernel,
        [shape((piece, width), BF), shape((piece, width), BF), shape((2 * piece, width), BF)],
        [keep, received],
        4,
    )
    beside, across = turn_beside(beside), turn_across(across)
    own_grad, half_grad = call(
        stream_kernel,
        [shape((2 * piece, width), BF), shape((piece, width), BF)],
        [own, swap(own), beside, swap(beside), across, swap(across), stream, gain, out_grad],
        4,
    )
    beside, across = turn_beside(own_grad), turn_across(half_grad)
    stream_grad, latent_t, latent_rows, delta = call(
        latent_kernel,
        [
            shape((rows, width), BF),
            shape((LAT, flat), BF),
            shape((flat, LAT), BF),
            shape((1, flat), F32),
        ],
        [
            own_grad,
            beside,
            swap(beside),
            across,
            swap(across),
            out_proj,
            value_up,
            latent_out,
        ],
        8,
        flops=2 * flat * VHEAD * (width + LAT),
        scratch=[pltpu.VMEM((rows, width), BF), pltpu.SemaphoreType.DMA((1,))],
        far_out=(0,),
    )

    def back(side, keys):
        (key_part,) = call(
            functools.partial(back_kernel, side),
            [shape((slots, width), BF)],
            [keys, probs, latent_t, latent_rows, delta, query_rows],
            8,
            flops=2 * half * flat * (2 * LAT + key_width),
        )
        return key_part

    key_received = swap(back(1, other))
    key_mine = back(0, mine)
    (key_sum,) = call(add_kernel, [shape((slots, width), BF)], [key_mine, key_received], 4)
    key_parts = exchange(key_sum.reshape(ctx_count, SLOTS, width))
    (query_grad_t,) = call(
        query_kernel,
        [shape((heads, key_width, rows), BF)],
        [mine, other, probs, latent_t, delta],
        16,
        flops=4 * half * flat * (key_width + LAT),
    )
    key_parts, query_grad_t = lax.optimization_barrier((key_parts, query_grad_t))
    query_grad = jnp.transpose(query_grad_t, (2, 0, 1))
    (key_own,) = call(
        sum_kernel, [shape((SLOTS, width), BF)], [key_parts.reshape(slots, width)], 8
    )
    (key_chip,) = call(
        join_kernel, [shape((2 * SLOTS, width), BF)], [key_own, swap(key_own)], 4
    )
    beside, across = turn_beside(key_chip), turn_across(key_own)
    (key_grad,) = call(
        final_kernel,
        [shape((key_count, key_width), BF)],
        [key_chip, beside, swap(beside), across, swap(across)],
        4,
        scratch=[pltpu.VMEM((4, 2 * SLOTS, width), F32)],
    )
    return (stream_grad, query_grad, key_grad)


def solution(mesh):
    fine = Mesh(mesh.devices.reshape(4, 4, 2, 4, 2), ("y", "x", "zl", "zh", "co"))
    exp = EXP
    both = CTX + exp
    placed = (
        P(CTX, exp, None),
        P(CTX, None),
        P(CTX),
        P(exp, None, None),
        P(exp, None, None),
        P(CTX, None),
        P(),
        P(CTX, None),
        P(CTX, None),
        P(both, None, None),
        P(both, None, None),
        P(both, None, None),
        P(CTX, None),
    )
    return jax.shard_map(
        shards,
        mesh=fine,
        in_specs=placed,
        out_specs=(P(CTX, None), P(CTX, exp, None), P(CTX, None)),
        check_vma=False,
    )
```

```python
import functools

import jax
import jax.numpy as jnp
from jax import lax
from jax.experimental import pallas as pl
from jax.experimental.pallas import tpu as pltpu
from jax.sharding import Mesh, PartitionSpec as P

LAT = 512
ROPE = 64
VHEAD = 128
PACK = 4
SLOTS = 8
TOP = 8
EPSILON = 1e-06
SCALE = (VHEAD + ROPE) ** (-0.5)
BF = jnp.bfloat16
F32 = jnp.float32
CTX = ("y", "x", "zl")
EXP = ("zh", "co")
MIB = 1 << 20


def dot(left, right):
    return jnp.dot(left, right, preferred_element_type=F32)


def contract_last(left, right):
    return lax.dot_general(left, right, (((1,), (1,)), ((), ())), preferred_element_type=F32)


def contract_first(left, right):
    return lax.dot_general(left, right, (((0,), (0,)), ((), ())), preferred_element_type=F32)


def call(body, outs, args, vmem_mib, flops=0, scratch=(), far=(), far_out=()):
    size = sum(a.size * a.dtype.itemsize for a in args) + sum(
        o.size * jnp.dtype(o.dtype).itemsize for o in outs
    )

    def place(away):
        return pl.BlockSpec(memory_space=pltpu.HBM if away else pltpu.VMEM)

    return pl.pallas_call(
        body,
        out_shape=tuple(outs),
        in_specs=[place(i in far) for i in range(len(args))],
        out_specs=tuple(place(i in far_out) for i in range(len(outs))),
        scratch_shapes=list(scratch),
        compiler_params=pltpu.CompilerParams(vmem_limit_bytes=vmem_mib * MIB),
        cost_estimate=pl.CostEstimate(flops=flops, bytes_accessed=size, transcendentals=0),
    )(*args)


def shape(dims, dtype):
    return jax.ShapeDtypeStruct(dims, dtype)


def position():
    core, group = lax.axis_index("co"), lax.axis_index("zh")
    return group * 2 + core, core, group


def spread(row_ref):
    rows = row_ref[...].astype(F32)
    return jnp.concatenate([rows[i : i + 1, :] for i in range(rows.shape[0])], axis=1)


def prep_kernel(exp_count, *refs):
    pos = position()
    far, (send_far, weight), held, arrived = refs[:6], refs[6:8], refs[8:14], refs[14]
    send, left = refs[15], refs[16]
    stores = []

    def leave(at, wide):
        lanes = pl.ds(at, wide)
        store = pltpu.make_async_copy(
            send.at[:, lanes], send_far.at[:, lanes], left.at[len(stores)]
        )
        store.start()
        stores.append(store)

    copies = [
        pltpu.make_async_copy(source, target, arrived.at[i])
        for i, (source, target) in enumerate(zip(far, held))
    ]
    for copy in copies:
        copy.start()
    ids, gates, stream, gain, out_grad, keys = held
    copies[0].wait()
    copies[1].wait()
    rows, width = stream.shape
    slots = weight.shape[0]
    place = lax.broadcasted_iota(jnp.int32, (slots, rows), 0)
    expert = (place // SLOTS) * exp_count + pos[0]
    member = jnp.zeros((slots, rows), F32)
    weighting = jnp.zeros((slots, rows), F32)
    for k in range(ids.shape[0]):
        hit = ids[k : k + 1, :] == expert
        member = jnp.where(hit, 1.0, member)
        weighting = jnp.where(hit, gates[k : k + 1, :], weighting)
    before = (
        lax.broadcasted_iota(jnp.int32, (rows, rows), 0)
        < lax.broadcasted_iota(jnp.int32, (rows, rows), 1)
    ).astype(F32).astype(BF)
    rank = dot(member.astype(BF), before)
    chosen = (member > 0.5) & (rank == (place % SLOTS).astype(F32))
    select = jnp.where(chosen, 1.0, 0.0).astype(BF)
    weight[...] = jnp.where(chosen, weighting, 0.0)
    step = width // 3
    copies[4].wait()
    for c in range(0, width, step):
        send[:, width + c : width + c + step] = dot(select, out_grad[:, c : c + step]).astype(BF)
        leave(width + c, step)
    copies[5].wait()
    count = keys.shape[0]
    row = lax.broadcasted_iota(jnp.int32, (SLOTS, count), 0)
    key = lax.broadcasted_iota(jnp.int32, (SLOTS, count), 1)
    parts, ropes = [], []
    for q in range(PACK):
        wanted = pos[1] * (count // 2) + q * SLOTS + row
        pick = jnp.where(key == wanted, 1.0, 0.0).astype(BF)
        parts.append(dot(pick, keys[:, :LAT]))
        ropes.append(dot(pick, keys[:, LAT:]))
    parts.append(jnp.concatenate(ropes, axis=1))
    at = 2 * width
    for part in parts:
        wide = part.shape[1]
        part = jnp.broadcast_to(part[None], (slots // SLOTS, SLOTS, wide))
        send[:, at : at + wide] = part.reshape(slots, wide).astype(BF)
        leave(at, wide)
        at += wide
    copies[2].wait()
    copies[3].wait()
    stream_f = stream[...].astype(F32)
    inv_rms = lax.rsqrt(jnp.mean(stream_f * stream_f, axis=1, keepdims=True) + EPSILON)
    normed = (stream_f * inv_rms * spread(gain)).astype(BF)
    for c in range(0, width, step):
        send[:, c : c + step] = dot(select, normed[:, c : c + step]).astype(BF)
        leave(c, step)
    for store in stores:
        store.wait()


def expert_kernel(rows, w_gate, w_up, w_down, grads_far, key_pack, grads, arrived):
    width = w_gate.shape[0]
    stores = [pltpu.make_async_copy(rows.at[:, 2 * width :], key_pack, arrived.at[0])]
    stores[0].start()
    act_gate = dot(rows[:, :width], w_gate[...])
    act_up = dot(rows[:, :width], w_up[...])
    hidden_back = contract_last(rows[:, width : 2 * width], w_down[...])
    sig = jax.nn.sigmoid(act_gate)
    gate_back = (hidden_back * act_up * sig * (1.0 + act_gate * (1.0 - sig))).astype(BF)
    up_back = (hidden_back * act_gate * sig).astype(BF)
    step = width // 3
    for c in range(0, width, step):
        grads[:, c : c + step] = (
            contract_last(gate_back, w_gate[c : c + step, :])
            + contract_last(up_back, w_up[c : c + step, :])
        ).astype(BF)
        lanes = pl.ds(c, step)
        stores.append(
            pltpu.make_async_copy(
                grads.at[:, lanes], grads_far.at[:, lanes], arrived.at[len(stores)]
            )
        )
        stores[-1].start()
    for store in stores:
        store.wait()


def order_kernel(weight, ordered):
    pos = position()
    w = weight[...]
    high = w.astype(BF)
    low = (w - high.astype(F32)).astype(BF)
    rows = w.shape[1]
    piece = rows // 8
    core, chip = pos[1], pos[2]
    place = lax.broadcasted_iota(jnp.int32, (1, rows), 1)
    part, within = (place // piece) % 4, place % piece
    side = jnp.where(place < rows // 2, core, 1 - core)
    at_chip = jnp.where(part == 0, chip, jnp.where(part == 1, chip + 3, chip + 2 - side)) % 4
    half = jnp.where(part < 2, side, part - 2)
    source = (at_chip * 2 + half) * piece + within
    index = lax.broadcasted_iota(jnp.int32, (rows, rows), 0)
    moved = jnp.where(index == source, 1.0, 0.0).astype(BF)
    slots = w.shape[0]
    for i, source in enumerate((high, low)):
        turned = lax.dot_general(
            moved, source, (((0,), (1,)), ((), ())), preferred_element_type=F32
        )
        ordered[:, i * slots : (i + 1) * slots] = turned.astype(BF)


def combine_kernel(returned, ordered, keep, send):
    half, width = keep.shape
    slots = returned.shape[0]
    step = width // 3
    for c in range(0, width, step):
        part = returned[:, c : c + step]
        total = dot(ordered[:, :slots], part) + dot(ordered[:, slots:], part)
        keep[:, c : c + step] = total[:half, :]
        send[:, c : c + step] = total[half:, :].astype(BF)


def pair_kernel(keep, received, own, near, far):
    total = (keep[...] + received[...].astype(F32)).astype(BF)
    piece = own.shape[0]
    own[...] = total[:piece, :]
    near[...] = total[piece : 2 * piece, :]
    far[...] = total[2 * piece :, :]


def stream_kernel(
    own, own_2, far, far_2, near, near_2, stream, gain, out_grad, stream_grad, half_grad
):
    pos = position()
    first = pos[1] == 0
    piece, width = own.shape
    rows = 2 * piece

    def ordered(mine, other):
        a, b = mine[...].astype(F32), other[...].astype(F32)
        return jnp.where(first, a, b), jnp.where(first, b, a)

    below, above = ordered(far, far_2)
    normed_grad = jnp.concatenate(ordered(own, own_2), axis=0) + below + above
    normed_grad = normed_grad + jnp.concatenate(ordered(near, near_2), axis=0)
    here = pl.ds(pl.multiple_of(pos[2] * rows, rows), rows)
    stream_f = stream[here, :].astype(F32)
    gain_f = spread(gain)
    inv_rms = lax.rsqrt(jnp.mean(stream_f * stream_f, axis=1, keepdims=True) + EPSILON)
    scaled = normed_grad * gain_f
    branch = inv_rms * scaled - stream_f * (inv_rms * inv_rms * inv_rms) * jnp.mean(
        scaled * stream_f, axis=1, keepdims=True
    )
    result = (out_grad[here, :].astype(F32) + branch).astype(BF)
    stream_grad[...] = result
    half_grad[...] = jnp.where(first, result[:piece, :], result[piece:, :])


def latent_kernel(
    own,
    far,
    far_2,
    near,
    near_2,
    out_proj,
    value_up,
    latent_out,
    stream_far,
    latent_t,
    latent_rows,
    delta,
    stream_grad,
    sent,
):
    _, core, chip = position()
    piece = near.shape[0]

    def put(value, place, side):
        at = pl.multiple_of((lax.rem(chip + place, 4) * 2 + side) * piece, piece)
        stream_grad[pl.ds(at, value.shape[0]), :] = value[...]

    put(own, 0, 0)
    put(far, 2 + core, 0)
    put(far_2, 3 - core, 0)
    put(near, 1, core)
    put(near_2, 1, 1 - core)
    store = pltpu.make_async_copy(stream_grad, stream_far, sent.at[0])
    store.start()
    heads, lat, vhead = value_up.shape
    count = stream_grad.shape[0]
    all_rows = stream_grad[...]
    for h in range(heads):
        head_t = contract_last(out_proj[h], all_rows).astype(BF)
        grad_t = dot(value_up[h], head_t).astype(BF)
        cols = slice(h * count, (h + 1) * count)
        latent_t[:, cols] = grad_t
        grad_f = grad_t.astype(F32)
        delta[:, cols] = jnp.sum(grad_f * latent_out[:, cols], axis=0, keepdims=True)
        latent_rows[cols, :] = grad_f.T.astype(BF)
    store.wait()


def rope_lanes(q):
    at = PACK * LAT + (q // 2) * 2 * ROPE
    return slice(at, at + 2 * ROPE)


def scores_kernel(
    mine_far,
    other_far,
    queries_t,
    seen,
    probs_far,
    latent_far,
    rows_far,
    mine,
    other,
    scratch,
    probs,
    latent_out,
    query_rows,
    arrived,
):
    pos = position()
    heads, width, rows = queries_t.shape
    slots = mine.shape[0]
    count = heads * rows
    loads = [
        pltpu.make_async_copy(mine_far, mine, arrived.at[0]),
        pltpu.make_async_copy(other_far, other, arrived.at[1]),
    ]
    for load in loads:
        load.start()
    blank = jnp.zeros((ROPE, count), BF)
    query = jnp.concatenate([queries_t[h] for h in range(heads)], axis=1)
    rope = query[LAT:, :]
    ropes = [jnp.concatenate([rope, blank], axis=0), jnp.concatenate([blank, rope], axis=0)]
    stacked = jnp.concatenate([query[:LAT, :]] + ropes, axis=0)
    query_rows[...] = stacked.astype(F32).T.astype(BF)
    stores = [pltpu.make_async_copy(query_rows, rows_far, arrived.at[2])]
    stores[0].start()
    last = jnp.concatenate([seen[...]] * heads, axis=1)
    place = lax.broadcasted_iota(jnp.int32, (slots, 1), 0)
    slot_key = (place // SLOTS) * (2 * PACK * SLOTS) + place % SLOTS
    top = jnp.full((1, count), -jnp.inf, F32)
    for side, keys in enumerate((mine, other)):
        loads[side].wait()
        core = pos[1] if side == 0 else 1 - pos[1]
        for q in range(PACK):
            s = dot(keys[:, q * LAT : (q + 1) * LAT], query[:LAT, :])
            s = (s + dot(keys[:, rope_lanes(q)], ropes[q % 2])) * SCALE
            key = slot_key + (core * (PACK * SLOTS) + q * SLOTS)
            s = jnp.where(key <= last, s, -jnp.inf)
            scratch[side * PACK + q] = s
            top = jnp.maximum(top, jnp.max(s, axis=0, keepdims=True))
    total = jnp.zeros((1, count), F32)
    for c in range(2 * PACK):
        e = jnp.exp(scratch[c] - top)
        scratch[c] = e
        total = total + jnp.sum(e, axis=0, keepdims=True)
    inverse = 1.0 / total
    for c in range(2 * PACK):
        q = c % PACK
        p = (scratch[c] * inverse).astype(BF)
        probs[c] = p
        store = pltpu.make_async_copy(probs.at[c], probs_far.at[c], arrived.at[3 + c])
        store.start()
        stores.append(store)
        part = contract_first((mine if c < PACK else other)[:, q * LAT : (q + 1) * LAT], p)
        if c == 0:
            latent_out[...] = part
        else:
            latent_out[...] += part
    store = pltpu.make_async_copy(latent_out, latent_far, arrived.at[3 + 2 * PACK])
    store.start()
    for store in stores + [store]:
        store.wait()


def score_gradient(keys, p, q, latent_t, delta):
    prob_grad = dot(keys[:, q * LAT : (q + 1) * LAT], latent_t)
    return (p.astype(F32) * (prob_grad - delta) * SCALE).astype(BF)


def back_kernel(side, keys, probs, latent_t, latent_rows, delta, query_rows, key_grad):
    part = []
    for q in range(PACK):
        p = probs[side * PACK + q]
        sg = score_gradient(keys, p, q, latent_t[...], delta[...])
        key_grad[:, q * LAT : (q + 1) * LAT] = (
            dot(sg, query_rows[:, :LAT]) + dot(p, latent_rows[...])
        ).astype(BF)
        at = LAT + (q % 2) * 2 * ROPE
        part.append(dot(sg, query_rows[:, at : at + 2 * ROPE]))
        if q % 2:
            key_grad[:, rope_lanes(q)] = (part[q - 1] + part[q]).astype(BF)


def query_kernel(mine, other, probs, latent_t, delta, out):
    heads, width, rows = out.shape
    for pair in range(heads // 2):
        cols = slice(2 * pair * rows, 2 * (pair + 1) * rows)
        total = rope = None
        for side, keys in enumerate((mine, other)):
            for q in range(PACK):
                p = probs[side * PACK + q, :, cols]
                sg = score_gradient(keys, p, q, latent_t[:, cols], delta[:, cols])
                lat_part = contract_first(keys[:, q * LAT : (q + 1) * LAT], sg)
                rope_part = contract_first(keys[:, rope_lanes(q)], sg)
                rope_part = rope_part[(q % 2) * ROPE : (q % 2 + 1) * ROPE, :]
                total = lat_part if total is None else total + lat_part
                rope = rope_part if rope is None else rope + rope_part
        for i in range(2):
            own = slice(i * rows, (i + 1) * rows)
            out[2 * pair + i] = jnp.concatenate([total[:, own], rope[:, own]], axis=0).astype(BF)


def add_kernel(left, right, out_far, out, sent):
    stores = []
    piece = out.shape[0] // 4
    for i in range(4):
        here = pl.ds(i * piece, piece)
        out[here, :] = (left[here, :].astype(F32) + right[here, :].astype(F32)).astype(BF)
        stores.append(pltpu.make_async_copy(out.at[here, :], out_far.at[here, :], sent.at[i]))
        stores[-1].start()
    for store in stores:
        store.wait()


def sum_kernel(parts, out):
    count, width = parts.shape
    spread = parts[...].astype(F32).reshape(count // SLOTS, SLOTS, width)
    out[...] = jnp.sum(spread, axis=0).astype(BF)


def join_kernel(own, near, out):
    pos = position()
    first = pos[1] == 0
    a, b = own[...].astype(F32), near[...].astype(F32)
    out[...] = jnp.concatenate([jnp.where(first, a, b), jnp.where(first, b, a)], axis=0).astype(BF)


def final_kernel(own, far, far_2, near, near_2, out, chips):
    pos = position()
    first, chip = pos[1] == 0, pos[2]
    a, b = near[...].astype(F32), near_2[...].astype(F32)
    chips[chip] = own[...].astype(F32)
    chips[lax.rem(chip + 2 + pos[1], 4)] = far[...].astype(F32)
    chips[lax.rem(chip + 3 - pos[1], 4)] = far_2[...].astype(F32)
    chips[lax.rem(chip + 1, 4)] = jnp.concatenate(
        [jnp.where(first, a, b), jnp.where(first, b, a)], axis=0
    )
    total = ((chips[0] + chips[1]) + chips[2]) + chips[3]
    rows = []
    for core in range(2):
        part = total[core * SLOTS : (core + 1) * SLOTS, :]
        for q in range(PACK):
            at = PACK * LAT + q * ROPE
            rows.append(
                jnp.concatenate([part[:, q * LAT : (q + 1) * LAT], part[:, at : at + ROPE]], axis=1)
            )
    out[...] = jnp.concatenate(rows, axis=0).astype(BF)


def swap(value):
    return lax.ppermute(value, "co", [(0, 1), (1, 0)])


def turn_far(value):
    steps = [(2 * z + c, 2 * ((z + 2 - c) % 4) + c) for z in range(4) for c in range(2)]
    return lax.ppermute(value, EXP, steps)


def turn_near(value):
    return lax.ppermute(value, "zh", [(z, (z + 3) % 4) for z in range(4)])


def exchange(value):
    return lax.all_to_all(value, CTX, split_axis=0, concat_axis=0, tiled=True)


def shards(
    queries,
    key_latents,
    query_pos,
    value_up,
    out_proj,
    stream,
    norm_gain,
    expert_ids,
    gate_weights,
    w_gate,
    w_up,
    w_down,
    out_grad,
):
    ctx_count = lax.axis_size(CTX)
    exp_count = lax.axis_size("zh") * lax.axis_size("co")
    rows, width = stream.shape
    slots = ctx_count * SLOTS
    gain = norm_gain.reshape(width // 128, 128)
    hidden = w_gate.shape[2]

    key_count, key_width = key_latents.shape
    send, weight = call(
        functools.partial(prep_kernel, exp_count),
        [shape((slots, 3 * width), BF), shape((slots, rows), F32)],
        [expert_ids.T, gate_weights.T, stream, gain, out_grad, key_latents],
        58,
        flops=4 * slots * rows * width,
        scratch=[
            pltpu.VMEM((TOP, rows), jnp.int32),
            pltpu.VMEM((TOP, rows), F32),
            pltpu.VMEM((rows, width), BF),
            pltpu.VMEM(gain.shape, BF),
            pltpu.VMEM((rows, width), BF),
            pltpu.VMEM((key_count, key_width), BF),
            pltpu.SemaphoreType.DMA((6,)),
            pltpu.VMEM((slots, 3 * width), BF),
            pltpu.SemaphoreType.DMA((7 + PACK,)),
        ],
        far=range(6),
        far_out=(0,),
    )
    arrived = exchange(send.reshape(ctx_count, SLOTS, 3 * width)).reshape(slots, 3 * width)
    grads, mine = call(
        expert_kernel,
        [shape((slots, width), BF), shape((slots, width), BF)],
        [arrived, w_gate[0], w_up[0], w_down[0]],
        12,
        flops=10 * slots * width * hidden,
        scratch=[
            pltpu.VMEM((slots, width), BF),
            pltpu.SemaphoreType.DMA((4,)),
        ],
        far_out=(0, 1),
    )
    returned = exchange(grads.reshape(ctx_count, SLOTS, width))
    other = swap(mine)
    heads = queries.shape[1]
    flat = heads * rows
    half = slots * PACK
    wide = LAT + 4 * ROPE
    probs, latent_out, query_rows = call(
        scores_kernel,
        [
            shape((2 * PACK, slots, flat), BF),
            shape((LAT, flat), F32),
            shape((flat, wide), BF),
        ],
        [mine, other, jnp.transpose(queries, (1, 2, 0)), query_pos.reshape(1, rows)],
        14,
        flops=4 * half * flat * (key_width + LAT),
        scratch=[
            pltpu.VMEM((slots, width), BF),
            pltpu.VMEM((slots, width), BF),
            pltpu.VMEM((2 * PACK, slots, flat), F32),
            pltpu.VMEM((2 * PACK, slots, flat), BF),
            pltpu.VMEM((LAT, flat), F32),
            pltpu.VMEM((flat, wide), BF),
            pltpu.SemaphoreType.DMA((4 + 2 * PACK,)),
        ],
        far=(0, 1),
        far_out=(0, 1, 2),
    )
    (ordered,) = call(order_kernel, [shape((rows, 2 * slots), BF)], [weight], 4)
    returned, probs, latent_out, query_rows, ordered = lax.optimization_barrier(
        (returned, probs, latent_out, query_rows, ordered)
    )
    returned = returned.reshape(slots, width)

    keep, other_part = call(
        combine_kernel,
        [shape((rows // 2, width), F32), shape((rows // 2, width), BF)],
        [returned, ordered],
        8,
        flops=8 * slots * rows * width,
    )
    received = swap(other_part)
    piece = rows // 8
    own, near, far = call(
        pair_kernel,
        [shape((piece, width), BF), shape((piece, width), BF), shape((2 * piece, width), BF)],
        [keep, received],
        4,
    )
    near, far = turn_near(near), turn_far(far)
    own_grad, half_grad = call(
        stream_kernel,
        [shape((2 * piece, width), BF), shape((piece, width), BF)],
        [own, swap(own), far, swap(far), near, swap(near), stream, gain, out_grad],
        4,
    )
    near, far = turn_near(half_grad), turn_far(own_grad)
    stream_grad, latent_t, latent_rows, delta = call(
        latent_kernel,
        [
            shape((rows, width), BF),
            shape((LAT, flat), BF),
            shape((flat, LAT), BF),
            shape((1, flat), F32),
        ],
        [
            own_grad,
            far,
            swap(far),
            near,
            swap(near),
            out_proj,
            value_up,
            latent_out,
        ],
        8,
        flops=2 * flat * VHEAD * (width + LAT),
        scratch=[pltpu.VMEM((rows, width), BF), pltpu.SemaphoreType.DMA((1,))],
        far_out=(0,),
    )

    def back(side, keys):
        (key_part,) = call(
            functools.partial(back_kernel, side),
            [shape((slots, width), BF)],
            [keys, probs, latent_t, latent_rows, delta, query_rows],
            8,
            flops=2 * half * flat * (2 * LAT + key_width),
        )
        return key_part

    key_received = swap(back(1, other))
    key_mine = back(0, mine)
    (key_sum,) = call(
        add_kernel,
        [shape((slots, width), BF)],
        [key_mine, key_received],
        8,
        scratch=[pltpu.VMEM((slots, width), BF), pltpu.SemaphoreType.DMA((4,))],
        far_out=(0,),
    )
    key_parts = exchange(key_sum.reshape(ctx_count, SLOTS, width))
    (query_grad_t,) = call(
        query_kernel,
        [shape((heads, key_width, rows), BF)],
        [mine, other, probs, latent_t, delta],
        16,
        flops=4 * half * flat * (key_width + LAT),
    )
    key_parts, query_grad_t = lax.optimization_barrier((key_parts, query_grad_t))
    query_grad = jnp.transpose(query_grad_t, (2, 0, 1))
    (key_own,) = call(
        sum_kernel, [shape((SLOTS, width), BF)], [key_parts.reshape(slots, width)], 8
    )
    (key_chip,) = call(
        join_kernel, [shape((2 * SLOTS, width), BF)], [key_own, swap(key_own)], 4
    )
    far, near = turn_far(key_chip), turn_near(key_own)
    (key_grad,) = call(
        final_kernel,
        [shape((key_count, key_width), BF)],
        [key_chip, far, swap(far), near, swap(near)],
        4,
        scratch=[pltpu.VMEM((4, 2 * SLOTS, width), F32)],
    )
    return (stream_grad, query_grad, key_grad)


def solution(mesh):
    fine = Mesh(mesh.devices.reshape(4, 4, 2, 4, 2), ("y", "x", "zl", "zh", "co"))
    exp = EXP
    both = CTX + exp
    placed = (
        P(CTX, exp, None),
        P(CTX, None),
        P(CTX),
        P(exp, None, None),
        P(exp, None, None),
        P(CTX, None),
        P(),
        P(CTX, None),
        P(CTX, None),
        P(both, None, None),
        P(both, None, None),
        P(both, None, None),
        P(CTX, None),
    )
    return jax.shard_map(
        shards,
        mesh=fine,
        in_specs=placed,
        out_specs=(P(CTX, None), P(CTX, exp, None), P(CTX, None)),
        check_vma=False,
    )
```

```python
import functools

import jax
import jax.numpy as jnp
from jax import lax
from jax.experimental import pallas as pl
from jax.experimental.pallas import tpu as pltpu
from jax.sharding import Mesh, PartitionSpec as P

LAT = 512
ROPE = 64
VHEAD = 128
PACK = 4
SLOTS = 8
TOP = 8
EPSILON = 1e-06
SCALE = (VHEAD + ROPE) ** (-0.5)
BF = jnp.bfloat16
F32 = jnp.float32
CTX = ("y", "x", "zl")
EXP = ("zh", "co")
MIB = 1 << 20


def dot(left, right):
    return jnp.dot(left, right, preferred_element_type=F32)


def contract_last(left, right):
    return lax.dot_general(left, right, (((1,), (1,)), ((), ())), preferred_element_type=F32)


def contract_first(left, right):
    return lax.dot_general(left, right, (((0,), (0,)), ((), ())), preferred_element_type=F32)


def call(body, outs, args, vmem_mib, flops=0, scratch=(), far=(), far_out=()):
    size = sum(a.size * a.dtype.itemsize for a in args) + sum(
        o.size * jnp.dtype(o.dtype).itemsize for o in outs
    )

    def place(away):
        return pl.BlockSpec(memory_space=pltpu.HBM if away else pltpu.VMEM)

    return pl.pallas_call(
        body,
        out_shape=tuple(outs),
        in_specs=[place(i in far) for i in range(len(args))],
        out_specs=tuple(place(i in far_out) for i in range(len(outs))),
        scratch_shapes=list(scratch),
        compiler_params=pltpu.CompilerParams(vmem_limit_bytes=vmem_mib * MIB),
        cost_estimate=pl.CostEstimate(flops=flops, bytes_accessed=size, transcendentals=0),
    )(*args)


def shape(dims, dtype):
    return jax.ShapeDtypeStruct(dims, dtype)


def position():
    core, group = lax.axis_index("co"), lax.axis_index("zh")
    return group * 2 + core, core, group


def spread(row_ref):
    rows = row_ref[...].astype(F32)
    return jnp.concatenate([rows[i : i + 1, :] for i in range(rows.shape[0])], axis=1)


def prep_kernel(exp_count, *refs):
    pos = position()
    far, (send_far, weight), held, arrived = refs[:6], refs[6:8], refs[8:14], refs[14]
    send, left = refs[15], refs[16]
    stores = []

    def leave(at, wide):
        lanes = pl.ds(at, wide)
        store = pltpu.make_async_copy(
            send.at[:, lanes], send_far.at[:, lanes], left.at[len(stores)]
        )
        store.start()
        stores.append(store)

    copies = [
        pltpu.make_async_copy(source, target, arrived.at[i])
        for i, (source, target) in enumerate(zip(far, held))
    ]
    for copy in copies:
        copy.start()
    ids, gates, stream, gain, out_grad, keys = held
    copies[0].wait()
    copies[1].wait()
    rows, width = stream.shape
    slots = weight.shape[0]
    place = lax.broadcasted_iota(jnp.int32, (slots, rows), 0)
    expert = (place // SLOTS) * exp_count + pos[0]
    member = jnp.zeros((slots, rows), F32)
    weighting = jnp.zeros((slots, rows), F32)
    for k in range(ids.shape[0]):
        hit = ids[k : k + 1, :] == expert
        member = jnp.where(hit, 1.0, member)
        weighting = jnp.where(hit, gates[k : k + 1, :], weighting)
    before = (
        lax.broadcasted_iota(jnp.int32, (rows, rows), 0)
        < lax.broadcasted_iota(jnp.int32, (rows, rows), 1)
    ).astype(F32).astype(BF)
    rank = dot(member.astype(BF), before)
    chosen = (member > 0.5) & (rank == (place % SLOTS).astype(F32))
    select = jnp.where(chosen, 1.0, 0.0).astype(BF)
    weight[...] = jnp.where(chosen, weighting, 0.0)
    step = width // 3
    copies[4].wait()
    for c in range(0, width, step):
        send[:, width + c : width + c + step] = dot(select, out_grad[:, c : c + step]).astype(BF)
        leave(width + c, step)
    copies[5].wait()
    count = keys.shape[0]
    row = lax.broadcasted_iota(jnp.int32, (SLOTS, count), 0)
    key = lax.broadcasted_iota(jnp.int32, (SLOTS, count), 1)
    parts, ropes = [], []
    for q in range(PACK):
        wanted = pos[1] * (count // 2) + q * SLOTS + row
        pick = jnp.where(key == wanted, 1.0, 0.0).astype(BF)
        parts.append(dot(pick, keys[:, :LAT]))
        ropes.append(dot(pick, keys[:, LAT:]))
    parts.append(jnp.concatenate(ropes, axis=1))
    at = 2 * width
    for part in parts:
        wide = part.shape[1]
        part = jnp.broadcast_to(part[None], (slots // SLOTS, SLOTS, wide))
        send[:, at : at + wide] = part.reshape(slots, wide).astype(BF)
        leave(at, wide)
        at += wide
    copies[2].wait()
    copies[3].wait()
    stream_f = stream[...].astype(F32)
    inv_rms = lax.rsqrt(jnp.mean(stream_f * stream_f, axis=1, keepdims=True) + EPSILON)
    normed = (stream_f * inv_rms * spread(gain)).astype(BF)
    for c in range(0, width, step):
        send[:, c : c + step] = dot(select, normed[:, c : c + step]).astype(BF)
        leave(c, step)
    for store in stores:
        store.wait()


def expert_kernel(rows, w_gate, w_up, w_down, grads_far, key_pack, grads, arrived):
    width = w_gate.shape[0]
    stores = [pltpu.make_async_copy(rows.at[:, 2 * width :], key_pack, arrived.at[0])]
    stores[0].start()
    act_gate = dot(rows[:, :width], w_gate[...])
    act_up = dot(rows[:, :width], w_up[...])
    hidden_back = contract_last(rows[:, width : 2 * width], w_down[...])
    sig = jax.nn.sigmoid(act_gate)
    gate_back = (hidden_back * act_up * sig * (1.0 + act_gate * (1.0 - sig))).astype(BF)
    up_back = (hidden_back * act_gate * sig).astype(BF)
    step = width // 3
    for c in range(0, width, step):
        grads[:, c : c + step] = (
            contract_last(gate_back, w_gate[c : c + step, :])
            + contract_last(up_back, w_up[c : c + step, :])
        ).astype(BF)
        lanes = pl.ds(c, step)
        stores.append(
            pltpu.make_async_copy(
                grads.at[:, lanes], grads_far.at[:, lanes], arrived.at[len(stores)]
            )
        )
        stores[-1].start()
    for store in stores:
        store.wait()


def order_kernel(weight, ordered):
    pos = position()
    w = weight[...]
    high = w.astype(BF)
    low = (w - high.astype(F32)).astype(BF)
    rows = w.shape[1]
    piece = rows // 8
    core, chip = pos[1], pos[2]
    place = lax.broadcasted_iota(jnp.int32, (1, rows), 1)
    part, within = (place // piece) % 4, place % piece
    side = jnp.where(place < rows // 2, core, 1 - core)
    at_chip = jnp.where(part == 0, chip, jnp.where(part == 1, chip + 3, chip + 2 - side)) % 4
    half = jnp.where(part < 2, side, part - 2)
    source = (at_chip * 2 + half) * piece + within
    index = lax.broadcasted_iota(jnp.int32, (rows, rows), 0)
    moved = jnp.where(index == source, 1.0, 0.0).astype(BF)
    slots = w.shape[0]
    for i, source in enumerate((high, low)):
        turned = lax.dot_general(
            moved, source, (((0,), (1,)), ((), ())), preferred_element_type=F32
        )
        ordered[:, i * slots : (i + 1) * slots] = turned.astype(BF)


def combine_kernel(part, returned, ordered, out):
    half, width = out.shape
    slots = returned.shape[0]
    rows = slice(part * half, (part + 1) * half)
    step = width // 3
    for c in range(0, width, step):
        block = returned[:, c : c + step]
        total = dot(ordered[rows, :slots], block) + dot(ordered[rows, slots:], block)
        out[:, c : c + step] = total.astype(out.dtype)


def pair_kernel(keep, received, own, near, far):
    total = (keep[...] + received[...].astype(F32)).astype(BF)
    piece = own.shape[0]
    own[...] = total[:piece, :]
    near[...] = total[piece : 2 * piece, :]
    far[...] = total[2 * piece :, :]


def stream_kernel(
    own, own_2, far, far_2, near, near_2, stream, gain, out_grad, stream_grad, half_grad
):
    pos = position()
    first = pos[1] == 0
    piece, width = own.shape
    rows = 2 * piece

    def ordered(mine, other):
        a, b = mine[...].astype(F32), other[...].astype(F32)
        return jnp.where(first, a, b), jnp.where(first, b, a)

    below, above = ordered(far, far_2)
    normed_grad = jnp.concatenate(ordered(own, own_2), axis=0) + below + above
    normed_grad = normed_grad + jnp.concatenate(ordered(near, near_2), axis=0)
    here = pl.ds(pl.multiple_of(pos[2] * rows, rows), rows)
    stream_f = stream[here, :].astype(F32)
    gain_f = spread(gain)
    inv_rms = lax.rsqrt(jnp.mean(stream_f * stream_f, axis=1, keepdims=True) + EPSILON)
    scaled = normed_grad * gain_f
    branch = inv_rms * scaled - stream_f * (inv_rms * inv_rms * inv_rms) * jnp.mean(
        scaled * stream_f, axis=1, keepdims=True
    )
    result = (out_grad[here, :].astype(F32) + branch).astype(BF)
    stream_grad[...] = result
    half_grad[...] = jnp.where(first, result[:piece, :], result[piece:, :])


def latent_kernel(
    own,
    far,
    far_2,
    near,
    near_2,
    out_proj,
    value_up,
    latent_out,
    stream_far,
    latent_t,
    latent_rows,
    delta,
    stream_grad,
    sent,
):
    _, core, chip = position()
    piece = near.shape[0]

    def put(value, place, side):
        at = pl.multiple_of((lax.rem(chip + place, 4) * 2 + side) * piece, piece)
        stream_grad[pl.ds(at, value.shape[0]), :] = value[...]

    put(own, 0, 0)
    put(far, 2 + core, 0)
    put(far_2, 3 - core, 0)
    put(near, 1, core)
    put(near_2, 1, 1 - core)
    store = pltpu.make_async_copy(stream_grad, stream_far, sent.at[0])
    store.start()
    heads, lat, vhead = value_up.shape
    count = stream_grad.shape[0]
    all_rows = stream_grad[...]
    for h in range(heads):
        head_t = contract_last(out_proj[h], all_rows).astype(BF)
        grad_t = dot(value_up[h], head_t).astype(BF)
        cols = slice(h * count, (h + 1) * count)
        latent_t[:, cols] = grad_t
        grad_f = grad_t.astype(F32)
        delta[:, cols] = jnp.sum(grad_f * latent_out[:, cols], axis=0, keepdims=True)
        latent_rows[cols, :] = grad_f.T.astype(BF)
    store.wait()


def rope_lanes(q):
    at = PACK * LAT + (q // 2) * 2 * ROPE
    return slice(at, at + 2 * ROPE)


def scores_kernel(
    mine_far,
    other_far,
    queries_t,
    seen,
    probs_far,
    latent_far,
    rows_far,
    mine,
    other,
    scratch,
    probs,
    latent_out,
    query_rows,
    arrived,
):
    pos = position()
    heads, width, rows = queries_t.shape
    slots = mine.shape[0]
    count = heads * rows
    loads = [
        pltpu.make_async_copy(mine_far, mine, arrived.at[0]),
        pltpu.make_async_copy(other_far, other, arrived.at[1]),
    ]
    for load in loads:
        load.start()
    blank = jnp.zeros((ROPE, count), BF)
    query = jnp.concatenate([queries_t[h] for h in range(heads)], axis=1)
    rope = query[LAT:, :]
    ropes = [jnp.concatenate([rope, blank], axis=0), jnp.concatenate([blank, rope], axis=0)]
    stacked = jnp.concatenate([query[:LAT, :]] + ropes, axis=0)
    query_rows[...] = stacked.astype(F32).T.astype(BF)
    stores = [pltpu.make_async_copy(query_rows, rows_far, arrived.at[2])]
    stores[0].start()
    last = jnp.concatenate([seen[...]] * heads, axis=1)
    place = lax.broadcasted_iota(jnp.int32, (slots, 1), 0)
    slot_key = (place // SLOTS) * (2 * PACK * SLOTS) + place % SLOTS
    top = jnp.full((1, count), -jnp.inf, F32)
    for side, keys in enumerate((mine, other)):
        loads[side].wait()
        core = pos[1] if side == 0 else 1 - pos[1]
        for q in range(PACK):
            s = dot(keys[:, q * LAT : (q + 1) * LAT], query[:LAT, :])
            s = (s + dot(keys[:, rope_lanes(q)], ropes[q % 2])) * SCALE
            key = slot_key + (core * (PACK * SLOTS) + q * SLOTS)
            s = jnp.where(key <= last, s, -jnp.inf)
            scratch[side * PACK + q] = s
            top = jnp.maximum(top, jnp.max(s, axis=0, keepdims=True))
    total = jnp.zeros((1, count), F32)
    for c in range(2 * PACK):
        e = jnp.exp(scratch[c] - top)
        scratch[c] = e
        total = total + jnp.sum(e, axis=0, keepdims=True)
    inverse = 1.0 / total
    for c in range(2 * PACK):
        q = c % PACK
        p = (scratch[c] * inverse).astype(BF)
        probs[c] = p
        store = pltpu.make_async_copy(probs.at[c], probs_far.at[c], arrived.at[3 + c])
        store.start()
        stores.append(store)
        part = contract_first((mine if c < PACK else other)[:, q * LAT : (q + 1) * LAT], p)
        if c == 0:
            latent_out[...] = part
        else:
            latent_out[...] += part
    store = pltpu.make_async_copy(latent_out, latent_far, arrived.at[3 + 2 * PACK])
    store.start()
    for store in stores + [store]:
        store.wait()


def score_gradient(keys, p, q, latent_t, delta):
    prob_grad = dot(keys[:, q * LAT : (q + 1) * LAT], latent_t)
    return (p.astype(F32) * (prob_grad - delta) * SCALE).astype(BF)


def back_kernel(side, keys, probs, latent_t, latent_rows, delta, query_rows, key_grad):
    part = []
    for q in range(PACK):
        p = probs[side * PACK + q]
        sg = score_gradient(keys, p, q, latent_t[...], delta[...])
        key_grad[:, q * LAT : (q + 1) * LAT] = (
            dot(sg, query_rows[:, :LAT]) + dot(p, latent_rows[...])
        ).astype(BF)
        at = LAT + (q % 2) * 2 * ROPE
        part.append(dot(sg, query_rows[:, at : at + 2 * ROPE]))
        if q % 2:
            key_grad[:, rope_lanes(q)] = (part[q - 1] + part[q]).astype(BF)


def query_kernel(mine, other, probs, latent_t, delta, out):
    heads, width, rows = out.shape
    for pair in range(heads // 2):
        cols = slice(2 * pair * rows, 2 * (pair + 1) * rows)
        total = rope = None
        for side, keys in enumerate((mine, other)):
            for q in range(PACK):
                p = probs[side * PACK + q, :, cols]
                sg = score_gradient(keys, p, q, latent_t[:, cols], delta[:, cols])
                lat_part = contract_first(keys[:, q * LAT : (q + 1) * LAT], sg)
                rope_part = contract_first(keys[:, rope_lanes(q)], sg)
                rope_part = rope_part[(q % 2) * ROPE : (q % 2 + 1) * ROPE, :]
                total = lat_part if total is None else total + lat_part
                rope = rope_part if rope is None else rope + rope_part
        for i in range(2):
            own = slice(i * rows, (i + 1) * rows)
            out[2 * pair + i] = jnp.concatenate([total[:, own], rope[:, own]], axis=0).astype(BF)


def add_kernel(left, right, out_far, out, sent):
    stores = []
    piece = out.shape[0] // 4
    for i in range(4):
        here = pl.ds(i * piece, piece)
        out[here, :] = (left[here, :].astype(F32) + right[here, :].astype(F32)).astype(BF)
        stores.append(pltpu.make_async_copy(out.at[here, :], out_far.at[here, :], sent.at[i]))
        stores[-1].start()
    for store in stores:
        store.wait()


def sum_kernel(parts, out):
    count, width = parts.shape
    spread = parts[...].astype(F32).reshape(count // SLOTS, SLOTS, width)
    out[...] = jnp.sum(spread, axis=0).astype(BF)


def join_kernel(own, near, out):
    pos = position()
    first = pos[1] == 0
    a, b = own[...].astype(F32), near[...].astype(F32)
    out[...] = jnp.concatenate([jnp.where(first, a, b), jnp.where(first, b, a)], axis=0).astype(BF)


def final_kernel(own, far, far_2, near, near_2, out, chips):
    pos = position()
    first, chip = pos[1] == 0, pos[2]
    a, b = near[...].astype(F32), near_2[...].astype(F32)
    chips[chip] = own[...].astype(F32)
    chips[lax.rem(chip + 2 + pos[1], 4)] = far[...].astype(F32)
    chips[lax.rem(chip + 3 - pos[1], 4)] = far_2[...].astype(F32)
    chips[lax.rem(chip + 1, 4)] = jnp.concatenate(
        [jnp.where(first, a, b), jnp.where(first, b, a)], axis=0
    )
    total = ((chips[0] + chips[1]) + chips[2]) + chips[3]
    rows = []
    for core in range(2):
        part = total[core * SLOTS : (core + 1) * SLOTS, :]
        for q in range(PACK):
            at = PACK * LAT + q * ROPE
            rows.append(
                jnp.concatenate([part[:, q * LAT : (q + 1) * LAT], part[:, at : at + ROPE]], axis=1)
            )
    out[...] = jnp.concatenate(rows, axis=0).astype(BF)


def swap(value):
    return lax.ppermute(value, "co", [(0, 1), (1, 0)])


def turn_far(value):
    steps = [(2 * z + c, 2 * ((z + 2 - c) % 4) + c) for z in range(4) for c in range(2)]
    return lax.ppermute(value, EXP, steps)


def turn_near(value):
    return lax.ppermute(value, "zh", [(z, (z + 3) % 4) for z in range(4)])


def exchange(value):
    return lax.all_to_all(value, CTX, split_axis=0, concat_axis=0, tiled=True)


def shards(
    queries,
    key_latents,
    query_pos,
    value_up,
    out_proj,
    stream,
    norm_gain,
    expert_ids,
    gate_weights,
    w_gate,
    w_up,
    w_down,
    out_grad,
):
    ctx_count = lax.axis_size(CTX)
    exp_count = lax.axis_size("zh") * lax.axis_size("co")
    rows, width = stream.shape
    slots = ctx_count * SLOTS
    gain = norm_gain.reshape(width // 128, 128)
    hidden = w_gate.shape[2]

    key_count, key_width = key_latents.shape
    send, weight = call(
        functools.partial(prep_kernel, exp_count),
        [shape((slots, 3 * width), BF), shape((slots, rows), F32)],
        [expert_ids.T, gate_weights.T, stream, gain, out_grad, key_latents],
        58,
        flops=4 * slots * rows * width,
        scratch=[
            pltpu.VMEM((TOP, rows), jnp.int32),
            pltpu.VMEM((TOP, rows), F32),
            pltpu.VMEM((rows, width), BF),
            pltpu.VMEM(gain.shape, BF),
            pltpu.VMEM((rows, width), BF),
            pltpu.VMEM((key_count, key_width), BF),
            pltpu.SemaphoreType.DMA((6,)),
            pltpu.VMEM((slots, 3 * width), BF),
            pltpu.SemaphoreType.DMA((7 + PACK,)),
        ],
        far=range(6),
        far_out=(0,),
    )
    arrived = exchange(send.reshape(ctx_count, SLOTS, 3 * width)).reshape(slots, 3 * width)
    grads, mine = call(
        expert_kernel,
        [shape((slots, width), BF), shape((slots, width), BF)],
        [arrived, w_gate[0], w_up[0], w_down[0]],
        12,
        flops=10 * slots * width * hidden,
        scratch=[
            pltpu.VMEM((slots, width), BF),
            pltpu.SemaphoreType.DMA((4,)),
        ],
        far_out=(0, 1),
    )
    returned = exchange(grads.reshape(ctx_count, SLOTS, width))
    other = swap(mine)
    heads = queries.shape[1]
    flat = heads * rows
    half = slots * PACK
    wide = LAT + 4 * ROPE
    probs, latent_out, query_rows = call(
        scores_kernel,
        [
            shape((2 * PACK, slots, flat), BF),
            shape((LAT, flat), F32),
            shape((flat, wide), BF),
        ],
        [mine, other, jnp.transpose(queries, (1, 2, 0)), query_pos.reshape(1, rows)],
        14,
        flops=4 * half * flat * (key_width + LAT),
        scratch=[
            pltpu.VMEM((slots, width), BF),
            pltpu.VMEM((slots, width), BF),
            pltpu.VMEM((2 * PACK, slots, flat), F32),
            pltpu.VMEM((2 * PACK, slots, flat), BF),
            pltpu.VMEM((LAT, flat), F32),
            pltpu.VMEM((flat, wide), BF),
            pltpu.SemaphoreType.DMA((4 + 2 * PACK,)),
        ],
        far=(0, 1),
        far_out=(0, 1, 2),
    )
    (ordered,) = call(order_kernel, [shape((rows, 2 * slots), BF)], [weight], 4)
    returned, probs, latent_out, query_rows, ordered = lax.optimization_barrier(
        (returned, probs, latent_out, query_rows, ordered)
    )
    returned = returned.reshape(slots, width)

    (other_part,) = call(
        functools.partial(combine_kernel, 1),
        [shape((rows // 2, width), BF)],
        [returned, ordered],
        8,
    )
    received = swap(other_part)
    (keep,) = call(
        functools.partial(combine_kernel, 0),
        [shape((rows // 2, width), F32)],
        [returned, ordered],
        8,
    )
    piece = rows // 8
    own, near, far = call(
        pair_kernel,
        [shape((piece, width), BF), shape((piece, width), BF), shape((2 * piece, width), BF)],
        [keep, received],
        4,
    )
    near, far = turn_near(near), turn_far(far)
    own_grad, half_grad = call(
        stream_kernel,
        [shape((2 * piece, width), BF), shape((piece, width), BF)],
        [own, swap(own), far, swap(far), near, swap(near), stream, gain, out_grad],
        4,
    )
    near, far = turn_near(half_grad), turn_far(own_grad)
    stream_grad, latent_t, latent_rows, delta = call(
        latent_kernel,
        [
            shape((rows, width), BF),
            shape((LAT, flat), BF),
            shape((flat, LAT), BF),
            shape((1, flat), F32),
        ],
        [
            own_grad,
            far,
            swap(far),
            near,
            swap(near),
            out_proj,
            value_up,
            latent_out,
        ],
        8,
        flops=2 * flat * VHEAD * (width + LAT),
        scratch=[pltpu.VMEM((rows, width), BF), pltpu.SemaphoreType.DMA((1,))],
        far_out=(0,),
    )

    def back(side, keys):
        (key_part,) = call(
            functools.partial(back_kernel, side),
            [shape((slots, width), BF)],
            [keys, probs, latent_t, latent_rows, delta, query_rows],
            8,
            flops=2 * half * flat * (2 * LAT + key_width),
        )
        return key_part

    key_received = swap(back(1, other))
    key_mine = back(0, mine)
    (key_sum,) = call(
        add_kernel,
        [shape((slots, width), BF)],
        [key_mine, key_received],
        8,
        scratch=[pltpu.VMEM((slots, width), BF), pltpu.SemaphoreType.DMA((4,))],
        far_out=(0,),
    )
    key_parts = exchange(key_sum.reshape(ctx_count, SLOTS, width))
    (query_grad_t,) = call(
        query_kernel,
        [shape((heads, key_width, rows), BF)],
        [mine, other, probs, latent_t, delta],
        16,
        flops=4 * half * flat * (key_width + LAT),
    )
    key_parts, query_grad_t = lax.optimization_barrier((key_parts, query_grad_t))
    query_grad = jnp.transpose(query_grad_t, (2, 0, 1))
    (key_own,) = call(
        sum_kernel, [shape((SLOTS, width), BF)], [key_parts.reshape(slots, width)], 8
    )
    (key_chip,) = call(
        join_kernel, [shape((2 * SLOTS, width), BF)], [key_own, swap(key_own)], 4
    )
    far, near = turn_far(key_chip), turn_near(key_own)
    (key_grad,) = call(
        final_kernel,
        [shape((key_count, key_width), BF)],
        [key_chip, far, swap(far), near, swap(near)],
        4,
        scratch=[pltpu.VMEM((4, 2 * SLOTS, width), F32)],
    )
    return (stream_grad, query_grad, key_grad)


def solution(mesh):
    fine = Mesh(mesh.devices.reshape(4, 4, 2, 4, 2), ("y", "x", "zl", "zh", "co"))
    exp = EXP
    both = CTX + exp
    placed = (
        P(CTX, exp, None),
        P(CTX, None),
        P(CTX),
        P(exp, None, None),
        P(exp, None, None),
        P(CTX, None),
        P(),
        P(CTX, None),
        P(CTX, None),
        P(both, None, None),
        P(both, None, None),
        P(both, None, None),
        P(CTX, None),
    )
    return jax.shard_map(
        shards,
        mesh=fine,
        in_specs=placed,
        out_specs=(P(CTX, None), P(CTX, exp, None), P(CTX, None)),
        check_vma=False,
    )
```

```python
import functools

import jax
import jax.numpy as jnp
from jax import lax
from jax.experimental import pallas as pl
from jax.experimental.pallas import tpu as pltpu
from jax.sharding import Mesh, PartitionSpec as P

LAT = 512
ROPE = 64
VHEAD = 128
PACK = 4
SLOTS = 8
TOP = 8
EPSILON = 1e-06
SCALE = (VHEAD + ROPE) ** (-0.5)
BF = jnp.bfloat16
F32 = jnp.float32
CTX = ("y", "x", "zl")
EXP = ("zh", "co")
MIB = 1 << 20


def dot(left, right):
    return jnp.dot(left, right, preferred_element_type=F32)


def contract_last(left, right):
    return lax.dot_general(left, right, (((1,), (1,)), ((), ())), preferred_element_type=F32)


def contract_first(left, right):
    return lax.dot_general(left, right, (((0,), (0,)), ((), ())), preferred_element_type=F32)


def call(body, outs, args, vmem_mib, flops=0, scratch=(), far=(), far_out=()):
    size = sum(a.size * a.dtype.itemsize for a in args) + sum(
        o.size * jnp.dtype(o.dtype).itemsize for o in outs
    )

    def place(away):
        return pl.BlockSpec(memory_space=pltpu.HBM if away else pltpu.VMEM)

    return pl.pallas_call(
        body,
        out_shape=tuple(outs),
        in_specs=[place(i in far) for i in range(len(args))],
        out_specs=tuple(place(i in far_out) for i in range(len(outs))),
        scratch_shapes=list(scratch),
        compiler_params=pltpu.CompilerParams(vmem_limit_bytes=vmem_mib * MIB),
        cost_estimate=pl.CostEstimate(flops=flops, bytes_accessed=size, transcendentals=0),
    )(*args)


def shape(dims, dtype):
    return jax.ShapeDtypeStruct(dims, dtype)


def position():
    core, group = lax.axis_index("co"), lax.axis_index("zh")
    return group * 2 + core, core, group


def spread(row_ref):
    rows = row_ref[...].astype(F32)
    return jnp.concatenate([rows[i : i + 1, :] for i in range(rows.shape[0])], axis=1)


def prep_kernel(exp_count, *refs):
    pos = position()
    far, (send_far, weight), held, arrived = refs[:6], refs[6:8], refs[8:14], refs[14]
    send, left = refs[15], refs[16]
    stores = []

    def leave(at, wide):
        lanes = pl.ds(at, wide)
        store = pltpu.make_async_copy(
            send.at[:, lanes], send_far.at[:, lanes], left.at[len(stores)]
        )
        store.start()
        stores.append(store)

    copies = [
        pltpu.make_async_copy(source, target, arrived.at[i])
        for i, (source, target) in enumerate(zip(far, held))
    ]
    for i in (5, 0, 1, 4, 2, 3):
        copies[i].start()
    ids, gates, stream, gain, out_grad, keys = held
    rows, width = stream.shape
    slots = weight.shape[0]
    copies[5].wait()
    count = keys.shape[0]
    row = lax.broadcasted_iota(jnp.int32, (SLOTS, count), 0)
    key = lax.broadcasted_iota(jnp.int32, (SLOTS, count), 1)
    parts, ropes = [], []
    for q in range(PACK):
        wanted = pos[1] * (count // 2) + q * SLOTS + row
        pick = jnp.where(key == wanted, 1.0, 0.0).astype(BF)
        parts.append(dot(pick, keys[:, :LAT]))
        ropes.append(dot(pick, keys[:, LAT:]))
    parts.append(jnp.concatenate(ropes, axis=1))
    at = 2 * width
    for part in parts:
        wide = part.shape[1]
        part = jnp.broadcast_to(part[None], (slots // SLOTS, SLOTS, wide))
        send[:, at : at + wide] = part.reshape(slots, wide).astype(BF)
        leave(at, wide)
        at += wide
    copies[0].wait()
    copies[1].wait()
    place = lax.broadcasted_iota(jnp.int32, (slots, rows), 0)
    expert = (place // SLOTS) * exp_count + pos[0]
    member = jnp.zeros((slots, rows), F32)
    weighting = jnp.zeros((slots, rows), F32)
    for k in range(ids.shape[0]):
        hit = ids[k : k + 1, :] == expert
        member = jnp.where(hit, 1.0, member)
        weighting = jnp.where(hit, gates[k : k + 1, :], weighting)
    before = (
        lax.broadcasted_iota(jnp.int32, (rows, rows), 0)
        < lax.broadcasted_iota(jnp.int32, (rows, rows), 1)
    ).astype(F32).astype(BF)
    rank = dot(member.astype(BF), before)
    chosen = (member > 0.5) & (rank == (place % SLOTS).astype(F32))
    select = jnp.where(chosen, 1.0, 0.0).astype(BF)
    weight[...] = jnp.where(chosen, weighting, 0.0)
    step = width // 3
    copies[4].wait()
    for c in range(0, width, step):
        send[:, width + c : width + c + step] = dot(select, out_grad[:, c : c + step]).astype(BF)
        leave(width + c, step)
    copies[2].wait()
    copies[3].wait()
    stream_f = stream[...].astype(F32)
    inv_rms = lax.rsqrt(jnp.mean(stream_f * stream_f, axis=1, keepdims=True) + EPSILON)
    normed = (stream_f * inv_rms * spread(gain)).astype(BF)
    for c in range(0, width, step):
        send[:, c : c + step] = dot(select, normed[:, c : c + step]).astype(BF)
        leave(c, step)
    for store in stores:
        store.wait()


def expert_kernel(rows, w_gate, w_up, w_down, grads_far, key_pack, grads, arrived):
    width = w_gate.shape[0]
    stores = [pltpu.make_async_copy(rows.at[:, 2 * width :], key_pack, arrived.at[0])]
    stores[0].start()
    act_gate = dot(rows[:, :width], w_gate[...])
    act_up = dot(rows[:, :width], w_up[...])
    hidden_back = contract_last(rows[:, width : 2 * width], w_down[...])
    sig = jax.nn.sigmoid(act_gate)
    gate_back = (hidden_back * act_up * sig * (1.0 + act_gate * (1.0 - sig))).astype(BF)
    up_back = (hidden_back * act_gate * sig).astype(BF)
    step = width // 3
    for c in range(0, width, step):
        grads[:, c : c + step] = (
            contract_last(gate_back, w_gate[c : c + step, :])
            + contract_last(up_back, w_up[c : c + step, :])
        ).astype(BF)
        lanes = pl.ds(c, step)
        stores.append(
            pltpu.make_async_copy(
                grads.at[:, lanes], grads_far.at[:, lanes], arrived.at[len(stores)]
            )
        )
        stores[-1].start()
    for store in stores:
        store.wait()


def order_kernel(weight, ordered):
    pos = position()
    w = weight[...]
    high = w.astype(BF)
    low = (w - high.astype(F32)).astype(BF)
    rows = w.shape[1]
    piece = rows // 8
    core, chip = pos[1], pos[2]
    place = lax.broadcasted_iota(jnp.int32, (1, rows), 1)
    part, within = (place // piece) % 4, place % piece
    side = jnp.where(place < rows // 2, core, 1 - core)
    at_chip = jnp.where(part == 0, chip, jnp.where(part == 1, chip + 3, chip + 2 - side)) % 4
    half = jnp.where(part < 2, side, part - 2)
    source = (at_chip * 2 + half) * piece + within
    index = lax.broadcasted_iota(jnp.int32, (rows, rows), 0)
    moved = jnp.where(index == source, 1.0, 0.0).astype(BF)
    slots = w.shape[0]
    for i, source in enumerate((high, low)):
        turned = lax.dot_general(
            moved, source, (((0,), (1,)), ((), ())), preferred_element_type=F32
        )
        ordered[:, i * slots : (i + 1) * slots] = turned.astype(BF)


def combine_kernel(part, returned, ordered, out):
    half, width = out.shape
    slots = returned.shape[0]
    rows = slice(part * half, (part + 1) * half)
    step = width // 3
    for c in range(0, width, step):
        block = returned[:, c : c + step]
        total = dot(ordered[rows, :slots], block) + dot(ordered[rows, slots:], block)
        out[:, c : c + step] = total.astype(out.dtype)


def pair_kernel(keep, received, own, near, far):
    total = (keep[...] + received[...].astype(F32)).astype(BF)
    piece = own.shape[0]
    own[...] = total[:piece, :]
    near[...] = total[piece : 2 * piece, :]
    far[...] = total[2 * piece :, :]


def stream_kernel(
    own, own_2, far, far_2, near, near_2, stream, gain, out_grad, stream_grad, half_grad
):
    pos = position()
    first = pos[1] == 0
    piece, width = own.shape
    rows = 2 * piece

    def ordered(mine, other):
        a, b = mine[...].astype(F32), other[...].astype(F32)
        return jnp.where(first, a, b), jnp.where(first, b, a)

    below, above = ordered(far, far_2)
    normed_grad = jnp.concatenate(ordered(own, own_2), axis=0) + below + above
    normed_grad = normed_grad + jnp.concatenate(ordered(near, near_2), axis=0)
    here = pl.ds(pl.multiple_of(pos[2] * rows, rows), rows)
    stream_f = stream[here, :].astype(F32)
    gain_f = spread(gain)
    inv_rms = lax.rsqrt(jnp.mean(stream_f * stream_f, axis=1, keepdims=True) + EPSILON)
    scaled = normed_grad * gain_f
    branch = inv_rms * scaled - stream_f * (inv_rms * inv_rms * inv_rms) * jnp.mean(
        scaled * stream_f, axis=1, keepdims=True
    )
    result = (out_grad[here, :].astype(F32) + branch).astype(BF)
    stream_grad[...] = result
    half_grad[...] = jnp.where(first, result[:piece, :], result[piece:, :])


def latent_kernel(
    own,
    far,
    far_2,
    near,
    near_2,
    out_proj,
    value_up,
    latent_out,
    stream_far,
    latent_t,
    latent_rows,
    delta,
    stream_grad,
    sent,
):
    _, core, chip = position()
    piece = near.shape[0]

    def put(value, place, side):
        at = pl.multiple_of((lax.rem(chip + place, 4) * 2 + side) * piece, piece)
        stream_grad[pl.ds(at, value.shape[0]), :] = value[...]

    put(own, 0, 0)
    put(far, 2 + core, 0)
    put(far_2, 3 - core, 0)
    put(near, 1, core)
    put(near_2, 1, 1 - core)
    store = pltpu.make_async_copy(stream_grad, stream_far, sent.at[0])
    store.start()
    heads, lat, vhead = value_up.shape
    count = stream_grad.shape[0]
    all_rows = stream_grad[...]
    for h in range(heads):
        head_t = contract_last(out_proj[h], all_rows).astype(BF)
        grad_t = dot(value_up[h], head_t).astype(BF)
        cols = slice(h * count, (h + 1) * count)
        latent_t[:, cols] = grad_t
        grad_f = grad_t.astype(F32)
        delta[:, cols] = jnp.sum(grad_f * latent_out[:, cols], axis=0, keepdims=True)
        latent_rows[cols, :] = grad_f.T.astype(BF)
    store.wait()


def rope_lanes(q):
    at = PACK * LAT + (q // 2) * 2 * ROPE
    return slice(at, at + 2 * ROPE)


def scores_kernel(
    mine_far,
    other_far,
    queries_t,
    seen,
    probs_far,
    latent_far,
    rows_far,
    mine,
    other,
    scratch,
    probs,
    latent_out,
    query_rows,
    arrived,
):
    pos = position()
    heads, width, rows = queries_t.shape
    slots = mine.shape[0]
    count = heads * rows
    loads = [
        pltpu.make_async_copy(mine_far, mine, arrived.at[0]),
        pltpu.make_async_copy(other_far, other, arrived.at[1]),
    ]
    for load in loads:
        load.start()
    blank = jnp.zeros((ROPE, count), BF)
    query = jnp.concatenate([queries_t[h] for h in range(heads)], axis=1)
    rope = query[LAT:, :]
    ropes = [jnp.concatenate([rope, blank], axis=0), jnp.concatenate([blank, rope], axis=0)]
    stacked = jnp.concatenate([query[:LAT, :]] + ropes, axis=0)
    query_rows[...] = stacked.astype(F32).T.astype(BF)
    stores = [pltpu.make_async_copy(query_rows, rows_far, arrived.at[2])]
    stores[0].start()
    last = jnp.concatenate([seen[...]] * heads, axis=1)
    place = lax.broadcasted_iota(jnp.int32, (slots, 1), 0)
    slot_key = (place // SLOTS) * (2 * PACK * SLOTS) + place % SLOTS
    top = jnp.full((1, count), -jnp.inf, F32)
    for side, keys in enumerate((mine, other)):
        loads[side].wait()
        core = pos[1] if side == 0 else 1 - pos[1]
        for q in range(PACK):
            s = dot(keys[:, q * LAT : (q + 1) * LAT], query[:LAT, :])
            s = (s + dot(keys[:, rope_lanes(q)], ropes[q % 2])) * SCALE
            key = slot_key + (core * (PACK * SLOTS) + q * SLOTS)
            s = jnp.where(key <= last, s, -jnp.inf)
            scratch[side * PACK + q] = s
            top = jnp.maximum(top, jnp.max(s, axis=0, keepdims=True))
    total = jnp.zeros((1, count), F32)
    for c in range(2 * PACK):
        e = jnp.exp(scratch[c] - top)
        scratch[c] = e
        total = total + jnp.sum(e, axis=0, keepdims=True)
    inverse = 1.0 / total
    for c in range(2 * PACK):
        q = c % PACK
        p = (scratch[c] * inverse).astype(BF)
        probs[c] = p
        store = pltpu.make_async_copy(probs.at[c], probs_far.at[c], arrived.at[3 + c])
        store.start()
        stores.append(store)
        part = contract_first((mine if c < PACK else other)[:, q * LAT : (q + 1) * LAT], p)
        if c == 0:
            latent_out[...] = part
        else:
            latent_out[...] += part
    store = pltpu.make_async_copy(latent_out, latent_far, arrived.at[3 + 2 * PACK])
    store.start()
    for store in stores + [store]:
        store.wait()


def score_gradient(keys, p, q, latent_t, delta):
    prob_grad = dot(keys[:, q * LAT : (q + 1) * LAT], latent_t)
    return (p.astype(F32) * (prob_grad - delta) * SCALE).astype(BF)


def back_kernel(side, keys, probs, latent_t, latent_rows, delta, query_rows, key_grad):
    part = []
    for q in range(PACK):
        p = probs[side * PACK + q]
        sg = score_gradient(keys, p, q, latent_t[...], delta[...])
        key_grad[:, q * LAT : (q + 1) * LAT] = (
            dot(sg, query_rows[:, :LAT]) + dot(p, latent_rows[...])
        ).astype(BF)
        at = LAT + (q % 2) * 2 * ROPE
        part.append(dot(sg, query_rows[:, at : at + 2 * ROPE]))
        if q % 2:
            key_grad[:, rope_lanes(q)] = (part[q - 1] + part[q]).astype(BF)


def query_kernel(mine, other, probs, latent_t, delta, out):
    heads, width, rows = out.shape
    for pair in range(heads // 2):
        cols = slice(2 * pair * rows, 2 * (pair + 1) * rows)
        total = rope = None
        for side, keys in enumerate((mine, other)):
            for q in range(PACK):
                p = probs[side * PACK + q, :, cols]
                sg = score_gradient(keys, p, q, latent_t[:, cols], delta[:, cols])
                lat_part = contract_first(keys[:, q * LAT : (q + 1) * LAT], sg)
                rope_part = contract_first(keys[:, rope_lanes(q)], sg)
                rope_part = rope_part[(q % 2) * ROPE : (q % 2 + 1) * ROPE, :]
                total = lat_part if total is None else total + lat_part
                rope = rope_part if rope is None else rope + rope_part
        for i in range(2):
            own = slice(i * rows, (i + 1) * rows)
            out[2 * pair + i] = jnp.concatenate([total[:, own], rope[:, own]], axis=0).astype(BF)


def add_kernel(left, right, out_far, out, sent):
    stores = []
    piece = out.shape[0] // 4
    for i in range(4):
        here = pl.ds(i * piece, piece)
        out[here, :] = (left[here, :].astype(F32) + right[here, :].astype(F32)).astype(BF)
        stores.append(pltpu.make_async_copy(out.at[here, :], out_far.at[here, :], sent.at[i]))
        stores[-1].start()
    for store in stores:
        store.wait()


def sum_kernel(parts, out):
    count, width = parts.shape
    spread = parts[...].astype(F32).reshape(count // SLOTS, SLOTS, width)
    out[...] = jnp.sum(spread, axis=0).astype(BF)


def join_kernel(own, near, out):
    pos = position()
    first = pos[1] == 0
    a, b = own[...].astype(F32), near[...].astype(F32)
    out[...] = jnp.concatenate([jnp.where(first, a, b), jnp.where(first, b, a)], axis=0).astype(BF)


def final_kernel(own, far, far_2, near, near_2, out, chips):
    pos = position()
    first, chip = pos[1] == 0, pos[2]
    a, b = near[...].astype(F32), near_2[...].astype(F32)
    chips[chip] = own[...].astype(F32)
    chips[lax.rem(chip + 2 + pos[1], 4)] = far[...].astype(F32)
    chips[lax.rem(chip + 3 - pos[1], 4)] = far_2[...].astype(F32)
    chips[lax.rem(chip + 1, 4)] = jnp.concatenate(
        [jnp.where(first, a, b), jnp.where(first, b, a)], axis=0
    )
    total = ((chips[0] + chips[1]) + chips[2]) + chips[3]
    rows = []
    for core in range(2):
        part = total[core * SLOTS : (core + 1) * SLOTS, :]
        for q in range(PACK):
            at = PACK * LAT + q * ROPE
            rows.append(
                jnp.concatenate([part[:, q * LAT : (q + 1) * LAT], part[:, at : at + ROPE]], axis=1)
            )
    out[...] = jnp.concatenate(rows, axis=0).astype(BF)


def swap(value):
    return lax.ppermute(value, "co", [(0, 1), (1, 0)])


def turn_far(value):
    steps = [(2 * z + c, 2 * ((z + 2 - c) % 4) + c) for z in range(4) for c in range(2)]
    return lax.ppermute(value, EXP, steps)


def turn_near(value):
    return lax.ppermute(value, "zh", [(z, (z + 3) % 4) for z in range(4)])


def exchange(value):
    return lax.all_to_all(value, CTX, split_axis=0, concat_axis=0, tiled=True)


def shards(
    queries,
    key_latents,
    query_pos,
    value_up,
    out_proj,
    stream,
    norm_gain,
    expert_ids,
    gate_weights,
    w_gate,
    w_up,
    w_down,
    out_grad,
):
    ctx_count = lax.axis_size(CTX)
    exp_count = lax.axis_size("zh") * lax.axis_size("co")
    rows, width = stream.shape
    slots = ctx_count * SLOTS
    gain = norm_gain.reshape(width // 128, 128)
    hidden = w_gate.shape[2]

    key_count, key_width = key_latents.shape
    send, weight = call(
        functools.partial(prep_kernel, exp_count),
        [shape((slots, 3 * width), BF), shape((slots, rows), F32)],
        [expert_ids.T, gate_weights.T, stream, gain, out_grad, key_latents],
        58,
        flops=4 * slots * rows * width,
        scratch=[
            pltpu.VMEM((TOP, rows), jnp.int32),
            pltpu.VMEM((TOP, rows), F32),
            pltpu.VMEM((rows, width), BF),
            pltpu.VMEM(gain.shape, BF),
            pltpu.VMEM((rows, width), BF),
            pltpu.VMEM((key_count, key_width), BF),
            pltpu.SemaphoreType.DMA((6,)),
            pltpu.VMEM((slots, 3 * width), BF),
            pltpu.SemaphoreType.DMA((7 + PACK,)),
        ],
        far=range(6),
        far_out=(0,),
    )
    arrived = exchange(send.reshape(ctx_count, SLOTS, 3 * width)).reshape(slots, 3 * width)
    grads, mine = call(
        expert_kernel,
        [shape((slots, width), BF), shape((slots, width), BF)],
        [arrived, w_gate[0], w_up[0], w_down[0]],
        12,
        flops=10 * slots * width * hidden,
        scratch=[
            pltpu.VMEM((slots, width), BF),
            pltpu.SemaphoreType.DMA((4,)),
        ],
        far_out=(0, 1),
    )
    returned = exchange(grads.reshape(ctx_count, SLOTS, width))
    other = swap(mine)
    heads = queries.shape[1]
    flat = heads * rows
    half = slots * PACK
    wide = LAT + 4 * ROPE
    probs, latent_out, query_rows = call(
        scores_kernel,
        [
            shape((2 * PACK, slots, flat), BF),
            shape((LAT, flat), F32),
            shape((flat, wide), BF),
        ],
        [mine, other, jnp.transpose(queries, (1, 2, 0)), query_pos.reshape(1, rows)],
        14,
        flops=4 * half * flat * (key_width + LAT),
        scratch=[
            pltpu.VMEM((slots, width), BF),
            pltpu.VMEM((slots, width), BF),
            pltpu.VMEM((2 * PACK, slots, flat), F32),
            pltpu.VMEM((2 * PACK, slots, flat), BF),
            pltpu.VMEM((LAT, flat), F32),
            pltpu.VMEM((flat, wide), BF),
            pltpu.SemaphoreType.DMA((4 + 2 * PACK,)),
        ],
        far=(0, 1),
        far_out=(0, 1, 2),
    )
    (ordered,) = call(order_kernel, [shape((rows, 2 * slots), BF)], [weight], 4)
    returned, probs, latent_out, query_rows, ordered = lax.optimization_barrier(
        (returned, probs, latent_out, query_rows, ordered)
    )
    returned = returned.reshape(slots, width)

    (other_part,) = call(
        functools.partial(combine_kernel, 1),
        [shape((rows // 2, width), BF)],
        [returned, ordered],
        8,
    )
    received = swap(other_part)
    (keep,) = call(
        functools.partial(combine_kernel, 0),
        [shape((rows // 2, width), F32)],
        [returned, ordered],
        8,
    )
    piece = rows // 8
    own, near, far = call(
        pair_kernel,
        [shape((piece, width), BF), shape((piece, width), BF), shape((2 * piece, width), BF)],
        [keep, received],
        4,
    )
    near, far = turn_near(near), turn_far(far)
    own_grad, half_grad = call(
        stream_kernel,
        [shape((2 * piece, width), BF), shape((piece, width), BF)],
        [own, swap(own), far, swap(far), near, swap(near), stream, gain, out_grad],
        4,
    )
    near, far = turn_near(half_grad), turn_far(own_grad)
    stream_grad, latent_t, latent_rows, delta = call(
        latent_kernel,
        [
            shape((rows, width), BF),
            shape((LAT, flat), BF),
            shape((flat, LAT), BF),
            shape((1, flat), F32),
        ],
        [
            own_grad,
            far,
            swap(far),
            near,
            swap(near),
            out_proj,
            value_up,
            latent_out,
        ],
        8,
        flops=2 * flat * VHEAD * (width + LAT),
        scratch=[pltpu.VMEM((rows, width), BF), pltpu.SemaphoreType.DMA((1,))],
        far_out=(0,),
    )

    def back(side, keys):
        (key_part,) = call(
            functools.partial(back_kernel, side),
            [shape((slots, width), BF)],
            [keys, probs, latent_t, latent_rows, delta, query_rows],
            8,
            flops=2 * half * flat * (2 * LAT + key_width),
        )
        return key_part

    key_received = swap(back(1, other))
    key_mine = back(0, mine)
    (key_sum,) = call(
        add_kernel,
        [shape((slots, width), BF)],
        [key_mine, key_received],
        8,
        scratch=[pltpu.VMEM((slots, width), BF), pltpu.SemaphoreType.DMA((4,))],
        far_out=(0,),
    )
    key_parts = exchange(key_sum.reshape(ctx_count, SLOTS, width))
    (query_grad_t,) = call(
        query_kernel,
        [shape((heads, key_width, rows), BF)],
        [mine, other, probs, latent_t, delta],
        16,
        flops=4 * half * flat * (key_width + LAT),
    )
    key_parts, query_grad_t = lax.optimization_barrier((key_parts, query_grad_t))
    query_grad = jnp.transpose(query_grad_t, (2, 0, 1))
    (key_own,) = call(
        sum_kernel, [shape((SLOTS, width), BF)], [key_parts.reshape(slots, width)], 8
    )
    (key_chip,) = call(
        join_kernel, [shape((2 * SLOTS, width), BF)], [key_own, swap(key_own)], 4
    )
    far, near = turn_far(key_chip), turn_near(key_own)
    (key_grad,) = call(
        final_kernel,
        [shape((key_count, key_width), BF)],
        [key_chip, far, swap(far), near, swap(near)],
        4,
        scratch=[pltpu.VMEM((4, 2 * SLOTS, width), F32)],
    )
    return (stream_grad, query_grad, key_grad)


def solution(mesh):
    fine = Mesh(mesh.devices.reshape(4, 4, 2, 4, 2), ("y", "x", "zl", "zh", "co"))
    exp = EXP
    both = CTX + exp
    placed = (
        P(CTX, exp, None),
        P(CTX, None),
        P(CTX),
        P(exp, None, None),
        P(exp, None, None),
        P(CTX, None),
        P(),
        P(CTX, None),
        P(CTX, None),
        P(both, None, None),
        P(both, None, None),
        P(both, None, None),
        P(CTX, None),
    )
    return jax.shard_map(
        shards,
        mesh=fine,
        in_specs=placed,
        out_specs=(P(CTX, None), P(CTX, exp, None), P(CTX, None)),
        check_vma=False,
    )
```
